128 devices in a mesh: rcv: 32 (over x, y, z_lo), src: 4 (over z_hi, core).
Axes of the slice: x: 4, y: 4, z: 4 (z_hi: 2, z_lo: 2; z = z_hi * 2 + z_lo), core: 2. Of those that a mesh axis runs over, the one named last changes fastest.
Arguments:
- record: bfloat16 [12800, 8192], P(('rcv', 'src')), may hold values from -6 to 6
- quality: int32 [8192], replicated, may hold values 0 or 1
- keep_flags: int32 [32, 8192], replicated, may hold values 0 or 1
- old_stacks: bfloat16 [401, 128, 8192], P(None, 'src', 'rcv'), may hold values from -4 to 4
Outputs:
- stacks: float32 [401, 128, 8192], P(None, 'src', 'rcv')
The draws below stay inside these ranges and needn't reach their ends.
All inputs are finite; a program needn't handle non-finite values.
Results may differ from the reference program's by a relative error of at most 0.0039.
Values may be sent and summed in bfloat16 or wider, within the bound.
No kernel may reach another device: no remote copies, remote signals or barrier semaphores. Data moves between devices by JAX's collectives and lax.ppermute only.
A program may use at most 192 MiB of HBM per device.

```python
import math
import jax
import jax.numpy as jnp
from jax import lax

WIN = 400
NFFT = 800
BINS = 401
LARGEST_LAG = 200
LAGS = 401
HALFBAND = 32
SUB = 32
RCV_DEV = 256
RECEIVERS = 8192
SOURCE_CHANNELS = 128
TIME = 12800


def set_ends(entries, stream_key, low, high):
    place = [jax.random.randint(jax.random.fold_in(stream_key, axis), (), 0, length) for axis, length in enumerate(entries.shape)]
    widest = entries.shape.index(max(entries.shape))
    neighbour = place[:widest] + [(place[widest] + 1) % entries.shape[widest]] + place[widest + 1:]
    return entries.at[tuple(place)].set(low).at[tuple(neighbour)].set(high)


def block_scale(own_key, dims, shards, least, top_value):
    loudness = 1.0
    for position, parts in shards:
        draws = jax.random.uniform(jax.random.fold_in(jax.random.fold_in(own_key, 6), position), (parts,), jnp.float32, least / len(shards), top_value / len(shards))
        loudness = loudness * jnp.repeat(jnp.exp(draws), dims[position] // parts).reshape((-1,) + (1,) * (len(dims) - 1 - position))
    return loudness


def noise(key, shape, width, most, pieces=(), kind=jnp.bfloat16):
    drawn = jax.random.normal(key, shape, jnp.float32) * width
    if len(pieces) > 0:
        drawn = block_scale(key, shape, pieces, -0.22, 0.18) * drawn
    return jnp.clip(drawn, min=-most, max=most).astype(kind)


def setup_inputs(seed: int = 0) -> dict:
    streams_of = jax.random.split(jax.random.key(seed), 5)
    record = noise(streams_of[0], (TIME, RECEIVERS), 1.0, 6.0, ((0, 128),))
    quality = set_ends((jax.random.randint(streams_of[1], (RECEIVERS,), 0, 4) < 3).astype(jnp.int32), jax.random.fold_in(streams_of[1], 1), 0, 1)
    keep_flags = set_ends((jax.random.randint(streams_of[2], (SUB, RECEIVERS), 0, 2) < 1).astype(jnp.int32), jax.random.fold_in(streams_of[2], 1), 0, 1)
    old_stacks = noise(streams_of[3], (LAGS, SOURCE_CHANNELS, RECEIVERS), 0.5, 4.0, ((1, 4), (2, 32)))
    return {"record": record, "quality": quality, "keep_flags": keep_flags, "old_stacks": old_stacks}


EPSILON = 1e-06

def forward_table():
    sample_ids = jnp.arange(WIN, dtype=jnp.int32)[:, None]
    bin_ids = jnp.arange(BINS, dtype=jnp.int32)[None, :]
    phases = (sample_ids * bin_ids % NFFT).astype(jnp.float32) * (2.0 * math.pi / NFFT)
    return jnp.concatenate([jnp.cos(phases), -jnp.sin(phases)], axis=1)

def band_table():
    bin_rows = jnp.arange(BINS, dtype=jnp.int32)[:, None]
    bin_cols = jnp.arange(BINS, dtype=jnp.int32)[None, :]
    inside = (jnp.abs(bin_rows - bin_cols) <= HALFBAND).astype(jnp.float32)
    counts = lax.optimization_barrier(jnp.sum(inside, axis=1, keepdims=True))
    return inside / (2.0 * counts)

def lag_table():
    lag_ids = jnp.arange(LAGS, dtype=jnp.int32)[:, None] - LARGEST_LAG
    bin_ids = jnp.arange(BINS, dtype=jnp.int32)[None, :]
    phases = (lag_ids * bin_ids % NFFT).astype(jnp.float32) * (2.0 * math.pi / NFFT)
    edges = jnp.logical_or(bin_ids == 0, bin_ids == NFFT // 2)
    weights = jnp.where(edges, 1.0, 2.0).astype(jnp.float32) / math.sqrt(NFFT)
    return jnp.concatenate([weights * jnp.cos(phases), -weights * jnp.sin(phases)], axis=1).astype(jnp.bfloat16)

def whiten(samples, channel_flags):
    channels = samples.shape[1]
    segment = samples.astype(jnp.float32).reshape(SUB, WIN, channels)
    segment = segment - lax.optimization_barrier(jnp.mean(segment, axis=1, keepdims=True))
    spectrum = jnp.einsum('swc,wg->sgc', segment, forward_table(), precision=lax.Precision.HIGHEST)
    real_part = spectrum[:, :BINS]
    imag_part = spectrum[:, BINS:]
    power_sum = real_part * real_part + imag_part * imag_part
    smooth = jnp.einsum('fg,sgc->sfc', band_table(), power_sum, precision=lax.Precision.HIGHEST)
    inverse_amp = channel_flags[:, None, :] / jnp.sqrt(smooth + EPSILON)
    return jnp.concatenate([real_part * inverse_amp, imag_part * inverse_amp], axis=1).astype(jnp.bfloat16)

def stack_update(sources, receivers, keep_src, keep_rcv, old_block):
    src_real = sources[:, :BINS].astype(jnp.float32)
    src_imag = sources[:, BINS:].astype(jnp.float32)
    rcv_real = receivers[:, :BINS].astype(jnp.float32)
    rcv_imag = receivers[:, BINS:].astype(jnp.float32)

    def product(left_operand, right_operand):
        return jnp.einsum('gxy,gxa->xya', left_operand, right_operand)
    cross_real = product(src_real, rcv_real) + product(src_imag, rcv_imag)
    cross_imag = product(src_real, rcv_imag) - product(src_imag, rcv_real)
    cross_spec = jnp.concatenate([cross_real, cross_imag], axis=0).astype(jnp.bfloat16)
    src_width = cross_spec.shape[1]
    rcv_width = cross_spec.shape[2]
    lagged = jnp.dot(lag_table(), cross_spec.reshape(2 * BINS, src_width * rcv_width), preferred_element_type=jnp.float32)
    lagged = lagged.reshape(LAGS, src_width, rcv_width)
    station_pair_count = jnp.dot(keep_src.T, keep_rcv, preferred_element_type=jnp.float32)
    return old_block.astype(jnp.float32) + lagged / jnp.maximum(station_pair_count, 1.0)[None]

def reference(record, quality, keep_flags, old_stacks):
    keep_all = keep_flags.astype(jnp.float32)
    channel_flags = keep_all * quality.astype(jnp.float32)[None, :]
    sources = whiten(record[:, :SOURCE_CHANNELS], channel_flags[:, :SOURCE_CHANNELS])
    keep_src = keep_all[:, :SOURCE_CHANNELS]
    blocks = RECEIVERS // RCV_DEV

    def one_block(index, stacks):
        offset = (index * RCV_DEV).astype(jnp.int32)
        rows = lax.dynamic_slice_in_dim(record, offset, RCV_DEV, 1)
        block_flags = lax.dynamic_slice_in_dim(channel_flags, offset, RCV_DEV, 1)
        keep_rcv = lax.dynamic_slice_in_dim(keep_all, offset, RCV_DEV, 1)
        old_block = lax.dynamic_slice_in_dim(old_stacks, offset, RCV_DEV, 2)
        receivers = whiten(rows, block_flags)
        updated = stack_update(sources, receivers, keep_src, keep_rcv, old_block)
        return lax.dynamic_update_slice_in_dim(stacks, updated, offset, 2)
    return lax.fori_loop(0, blocks, one_block, jnp.zeros((LAGS, SOURCE_CHANNELS, RECEIVERS), jnp.float32))
```

```python
import functools
import math

import jax
import jax.numpy as jnp
import numpy as np
from jax import lax
from jax.experimental import pallas as pl
from jax.experimental.pallas import tpu as pltpu
from jax.sharding import PartitionSpec as P

WIN = 400
NFFT = 800
BINS = 401
LARGEST_LAG = 200
LAGS = 401
HALFBAND = 32
SUB = 32
EPSILON = 1e-06

PIECE = WIN // 4
PADDED = 112
DEPTH = 4 * PADDED
FREQ = 416
HALF = 128
SRC = 64
OWN = 32
SHIFTS = 208
PITCH = 72
ROWS = 2 * SRC
XPITCH = ROWS + 8
BLOCK = 16
VMEM = 56 * 1024 * 1024


def split(table):
    high = table.astype(jnp.bfloat16)
    low = (table - high.astype(np.float32)).astype(jnp.bfloat16)
    return high, low


def forward_table():
    samples = np.arange(WIN)[None, :]
    bins = np.arange(BINS)[:, None]
    phases = (samples * bins % NFFT) * (2.0 * math.pi / NFFT)
    table = np.zeros((2, FREQ, 4, PADDED), np.float32)
    table[0, :BINS, :, :PIECE] = np.cos(phases).reshape(BINS, 4, PIECE)
    table[1, :BINS, :, :PIECE] = -np.sin(phases).reshape(BINS, 4, PIECE)
    high, low = split(table.reshape(2 * FREQ, DEPTH))
    sums = (high.astype(np.float64) + low.astype(np.float64)).sum(axis=1, keepdims=True)
    return high, low, np.broadcast_to((sums / WIN).astype(np.float32), (2 * FREQ, HALF)).copy()


def band_table():
    bins = np.arange(FREQ)
    inside = np.abs(bins[:, None] - bins[None, :]) <= HALFBAND
    inside &= (bins[:, None] < BINS) & (bins[None, :] < BINS)
    counts = np.maximum(inside.sum(axis=1, keepdims=True), 1)
    inverse = np.broadcast_to((1.0 / (2.0 * counts)).astype(np.float32), (FREQ, HALF)).copy()
    return inside.astype(jnp.bfloat16), inverse


def lag_tables():
    shifts = np.arange(LARGEST_LAG + 1)[:, None]
    bins = np.arange(BINS)[None, :]
    phases = (shifts * bins % NFFT) * (2.0 * math.pi / NFFT)
    weights = np.where((bins == 0) | (bins == NFFT // 2), 1.0, 2.0) / math.sqrt(NFFT)
    tables = np.zeros((2, SHIFTS, FREQ), np.float32)
    tables[0, : LARGEST_LAG + 1, :BINS] = weights * np.cos(phases)
    tables[1, : LARGEST_LAG + 1, :BINS] = -weights * np.sin(phases)
    return tables.astype(jnp.bfloat16)


def dot(a, b):
    return jnp.dot(a, b, preferred_element_type=jnp.float32)


def whiten_pair(x_ref, flag_ref, high_ref, low_ref, sums_ref, band_ref, inverse_ref, spec):
    x = jnp.concatenate([x_ref[0], x_ref[1]], axis=1)
    spec[...] = dot(high_ref[...], x) + dot(low_ref[...], x)
    total = spec[0:1, :]
    sums = sums_ref[...]
    sums = jnp.concatenate([sums, sums], axis=1)
    real = spec[:FREQ] - sums[:FREQ] * total
    imag = spec[FREQ:] - sums[FREQ:] * total
    power = real * real + imag * imag
    power_high = power.astype(jnp.bfloat16)
    power_low = (power - power_high.astype(jnp.float32)).astype(jnp.bfloat16)
    band = band_ref[...]
    smooth = dot(band, power_high) + dot(band, power_low)
    inverse = inverse_ref[...]
    inverse = jnp.concatenate([inverse, inverse], axis=1)
    flags = jnp.concatenate([flag_ref[0], flag_ref[1]], axis=1)
    scale = flags * lax.rsqrt(smooth * inverse + EPSILON)
    return real * scale, imag * scale


def whiten_sources_kernel(x_ref, flag_ref, high_ref, low_ref, sums_ref, band_ref, inverse_ref, out_ref, spec):
    real, imag = whiten_pair(x_ref, flag_ref, high_ref, low_ref, sums_ref, band_ref, inverse_ref, spec)
    for g in range(2):
        out_ref[g, 0] = real[:, g * HALF : (g + 1) * HALF].astype(jnp.bfloat16)
        out_ref[g, 1] = imag[:, g * HALF : (g + 1) * HALF].astype(jnp.bfloat16)


def whiten_receivers_kernel(x_ref, flag_ref, high_ref, low_ref, sums_ref, band_ref, inverse_ref, out_ref, spec, held):
    step = pl.program_id(0)
    real, imag = whiten_pair(x_ref, flag_ref, high_ref, low_ref, sums_ref, band_ref, inverse_ref, spec)
    for g in range(2):
        window = 2 * step + g
        held[pl.ds(window, FREQ, stride=PITCH), :] = real[:, g * HALF : (g + 1) * HALF]
        held[pl.ds(SUB + window, FREQ, stride=PITCH), :] = imag[:, g * HALF : (g + 1) * HALF]

    @pl.when(step == pl.num_programs(0) - 1)
    def _():
        @pl.loop(0, FREQ // 8)
        def _(block):
            for i in range(8):
                f = block * 8 + i
                out_ref[f] = held[pl.ds(pl.multiple_of(f * PITCH, 8), 2 * SUB), :].astype(jnp.bfloat16)


def whole(shape):
    return pl.BlockSpec(shape, lambda *_: (0,) * len(shape))


def whiten_call(kernel, x, flags, out_shape, out_spec, scratch):
    groups = x.shape[0]
    high, low, sums = forward_table()
    band, inverse = band_table()
    return pl.pallas_call(
        kernel,
        grid=(groups // 2,),
        in_specs=[
            pl.BlockSpec((2, DEPTH, HALF), lambda g: (g, 0, 0)),
            pl.BlockSpec((2, 1, HALF), lambda g: (g, 0, 0)),
            whole(high.shape),
            whole(low.shape),
            whole(sums.shape),
            whole(band.shape),
            whole(inverse.shape),
        ],
        out_specs=out_spec,
        out_shape=out_shape,
        scratch_shapes=[pltpu.VMEM((2 * FREQ, 2 * HALF), jnp.float32)] + scratch,
        compiler_params=pltpu.CompilerParams(vmem_limit_bytes=VMEM),
        cost_estimate=pl.CostEstimate(
            flops=groups * 2 * 2 * 2 * FREQ * DEPTH * HALF, bytes_accessed=groups * DEPTH * HALF * 6, transcendentals=0
        ),
    )(x, flags, jnp.asarray(high), jnp.asarray(low), jnp.asarray(sums), jnp.asarray(band), jnp.asarray(inverse))


def whiten_receivers(x, flags):
    return whiten_call(
        whiten_receivers_kernel,
        x,
        flags,
        jax.ShapeDtypeStruct((FREQ, 2 * SUB, HALF), jnp.bfloat16),
        whole((FREQ, 2 * SUB, HALF)),
        [pltpu.VMEM((FREQ * PITCH, HALF), jnp.float32)],
    )


def whiten_sources(x, flags):
    groups = x.shape[0]
    return whiten_call(
        whiten_sources_kernel,
        x,
        flags,
        jax.ShapeDtypeStruct((groups, 2, FREQ, HALF), jnp.bfloat16),
        pl.BlockSpec((2, 2, FREQ, HALF), lambda g: (g, 0, 0, 0)),
        [],
    )


def cross_kernel(left_ref, right_ref, out_ref, held):
    zeros = jnp.zeros((2 * SUB, HALF), jnp.bfloat16)
    for pair in range(BLOCK // 2):
        first = right_ref[2 * pair]
        second = right_ref[2 * pair + 1]
        weights = jnp.concatenate(
            [jnp.concatenate([first, zeros], axis=1), jnp.concatenate([zeros, second], axis=1)], axis=0
        )
        product = dot(left_ref[pair], weights)
        held[pl.ds(2 * pair * XPITCH, ROWS), :] = product[:, :HALF]
        held[pl.ds((2 * pair + 1) * XPITCH, ROWS), :] = product[:, HALF:]
    for row in range(ROWS):
        out_ref[row] = held[pl.ds(row, BLOCK, stride=XPITCH), :].astype(jnp.bfloat16)


def cross(left, right):
    return pl.pallas_call(
        cross_kernel,
        grid=(FREQ // BLOCK,),
        in_specs=[
            pl.BlockSpec((BLOCK // 2, ROWS, 4 * SUB), lambda f: (f, 0, 0)),
            pl.BlockSpec((BLOCK, 2 * SUB, HALF), lambda f: (f, 0, 0)),
        ],
        out_specs=pl.BlockSpec((ROWS, BLOCK, HALF), lambda f: (0, f, 0)),
        out_shape=jax.ShapeDtypeStruct((ROWS, FREQ, HALF), jnp.bfloat16),
        scratch_shapes=[pltpu.VMEM((BLOCK * XPITCH, HALF), jnp.float32)],
        compiler_params=pltpu.CompilerParams(vmem_limit_bytes=VMEM),
        cost_estimate=pl.CostEstimate(flops=FREQ * ROWS * 4 * SUB * 2 * HALF, bytes_accessed=30 << 20, transcendentals=0),
    )(left, right)


def lag_sums(real_ref, imag_ref, tables_ref, even, odd):
    for pair in range(BLOCK // 2):
        real = jnp.concatenate([real_ref[2 * pair], real_ref[2 * pair + 1]], axis=1)
        imag = jnp.concatenate([imag_ref[2 * pair], imag_ref[2 * pair + 1]], axis=1)
        cosine = dot(tables_ref[0], real)
        sine = dot(tables_ref[1], imag)
        for i in range(2):
            rows = pl.ds(2 * pair + i, SHIFTS, stride=BLOCK)
            even[rows, :] = cosine[:, i * HALF : (i + 1) * HALF]
            odd[rows, :] = sine[:, i * HALF : (i + 1) * HALF]


def shift_rows(m):
    return pl.ds(pl.multiple_of(m * BLOCK, BLOCK), BLOCK)


def lag_partner_kernel(place_ref, real_ref, imag_ref, tables_ref, count_ref, out_ref, even, odd):
    lag_sums(real_ref, imag_ref, tables_ref, even, odd)

    @pl.loop(0, LARGEST_LAG + 1, unroll=3)
    def _(m):
        e, o = even[shift_rows(m), :], odd[shift_rows(m), :]
        out_ref[LARGEST_LAG + m] = ((e + o) * count_ref[...]).astype(jnp.bfloat16)
        out_ref[LARGEST_LAG - m] = ((e - o) * count_ref[...]).astype(jnp.bfloat16)


def lag_own_kernel(place_ref, real_ref, imag_ref, tables_ref, count_ref, old_ref, out_ref, even, odd):
    lag_sums(real_ref, imag_ref, tables_ref, even, odd)

    @pl.loop(0, LARGEST_LAG + 1, unroll=3)
    def _(m):
        e, o = even[shift_rows(m), :], odd[shift_rows(m), :]
        above, below = LARGEST_LAG + m, LARGEST_LAG - m
        out_ref[above] = old_ref[above].astype(jnp.float32) + (e + o) * count_ref[...]
        out_ref[below] = old_ref[below].astype(jnp.float32) + (e - o) * count_ref[...]


def lag_call(kernel, place, spectra, inverse_count, old, half):
    steps = OWN // BLOCK
    tables = lag_tables()
    in_specs = [
        pl.BlockSpec((BLOCK, FREQ, HALF), lambda g, place: (half(place) * steps + g, 0, 0)),
        pl.BlockSpec((BLOCK, FREQ, HALF), lambda g, place: (SRC // BLOCK + half(place) * steps + g, 0, 0)),
        pl.BlockSpec(tables.shape, lambda g, place: (0, 0, 0)),
        pl.BlockSpec((BLOCK, HALF), lambda g, place: (half(place) * steps + g, 0)),
    ]
    operands = [spectra, spectra, jnp.asarray(tables), inverse_count]
    if old is None:
        out_shape = jax.ShapeDtypeStruct((LAGS, OWN, HALF), jnp.bfloat16)
        out_spec = pl.BlockSpec((LAGS, BLOCK, HALF), lambda g, place: (0, g, 0))
    else:
        in_specs.append(pl.BlockSpec((LAGS, BLOCK, HALF), lambda g, place: (0, g, place[0])))
        operands.append(old)
        out_shape = jax.ShapeDtypeStruct((LAGS, OWN, 2 * HALF), jnp.float32)
        out_spec = pl.BlockSpec((LAGS, BLOCK, HALF), lambda g, place: (0, g, place[0]))
    return pl.pallas_call(
        kernel,
        grid_spec=pltpu.PrefetchScalarGridSpec(
            num_scalar_prefetch=1,
            grid=(steps,),
            in_specs=in_specs,
            out_specs=out_spec,
            scratch_shapes=[pltpu.VMEM((SHIFTS * BLOCK, HALF), jnp.float32)] * 2,
        ),
        out_shape=out_shape,
        compiler_params=pltpu.CompilerParams(vmem_limit_bytes=VMEM),
        cost_estimate=pl.CostEstimate(flops=OWN * SHIFTS * FREQ * HALF * 4, bytes_accessed=16 << 20, transcendentals=0),
    )(place, *operands)


def merge_kernel(place_ref, held_ref, got_ref, old_ref, out_ref):
    out_ref[...] = old_ref[...].astype(jnp.float32) + got_ref[...].astype(jnp.float32)


def merge(place, stacks, got, old):
    rows = 58
    spec = pl.BlockSpec((rows, OWN, HALF), lambda l, place: (l, 0, 1 - place[0]))
    return pl.pallas_call(
        merge_kernel,
        grid_spec=pltpu.PrefetchScalarGridSpec(
            num_scalar_prefetch=1,
            grid=(pl.cdiv(LAGS, rows),),
            in_specs=[
                pl.BlockSpec(memory_space=pl.ANY),
                pl.BlockSpec((rows, OWN, HALF), lambda l, place: (l, 0, 0)),
                spec,
            ],
            out_specs=spec,
        ),
        out_shape=jax.ShapeDtypeStruct(stacks.shape, stacks.dtype),
        input_output_aliases={1: 0},
        compiler_params=pltpu.CompilerParams(vmem_limit_bytes=VMEM),
        cost_estimate=pl.CostEstimate(flops=LAGS * OWN * HALF, bytes_accessed=13 << 20, transcendentals=0),
    )(place, stacks, got, old)


def source_operand(whitened):
    x = whitened.reshape(SUB // 2, 2, FREQ // 2, 2, 2, SRC)
    real = x.transpose(2, 5, 3, 1, 0, 4)
    imag = jnp.concatenate([-real[:, :, :, 1:], real[:, :, :, :1]], axis=3)
    return jnp.concatenate([real, imag], axis=1).reshape(FREQ // 2, ROWS, 4 * SUB)


def on_device(record, quality, keep_flags, old_stacks):
    row = lax.axis_index("rcv")
    col = lax.axis_index("src")
    core = lax.rem(col, 2)
    chip = lax.div(col, 2)
    place = jnp.reshape(core, (1,)).astype(jnp.int32)
    blocks = lax.axis_size("rcv")

    padded = jnp.pad(record, ((0, PADDED - PIECE), (0, 0)))
    pieces = padded.reshape(PADDED, blocks, 1, 2, HALF).transpose(1, 2, 3, 0, 4)
    pieces = jnp.broadcast_to(pieces, (blocks, 2, 2, PADDED, HALF)).reshape(4 * blocks, PADDED, HALF)
    source_pieces = padded[:, : 2 * SRC].reshape(PADDED, 1, 2, 1, SRC).transpose(1, 2, 3, 0, 4)
    source_pieces = jnp.broadcast_to(source_pieces, (blocks, 2, 2, PADDED, SRC)).reshape(4 * blocks, PADDED, SRC)

    sources = lax.all_to_all(source_pieces, ("rcv", "src"), split_axis=0, concat_axis=0, tiled=True)
    receivers = lax.all_to_all(pieces, ("rcv", "src"), split_axis=0, concat_axis=0, tiled=True)

    keep_all = keep_flags.astype(jnp.float32)
    flags = keep_all * quality.astype(jnp.float32)[None, :]
    first_receiver = row * 2 * HALF + core * HALF
    keep_src = lax.dynamic_slice_in_dim(keep_all, chip * SRC, SRC, 1)
    keep_rcv = lax.dynamic_slice_in_dim(keep_all, first_receiver, HALF, 1)
    inverse_count = 1.0 / jnp.maximum(dot(keep_src.T, keep_rcv), 1.0)
    flags_src = lax.dynamic_slice_in_dim(flags, chip * SRC, SRC, 1).reshape(SUB // 2, 1, 2 * SRC)
    flags_rcv = lax.dynamic_slice_in_dim(flags, first_receiver, HALF, 1).reshape(SUB, 1, HALF)

    sources = sources.reshape(SUB // 2, 2, DEPTH, SRC).transpose(0, 2, 1, 3).reshape(SUB // 2, DEPTH, 2 * SRC)
    left = source_operand(whiten_sources(sources, flags_src))
    right = whiten_receivers(receivers.reshape(SUB, DEPTH, HALF), flags_rcv)
    spectra = cross(left, right)
    away = lag_call(lag_partner_kernel, place, spectra, inverse_count, None, lambda place: 1 - place[0])
    got = lax.ppermute(away, "src", [(0, 1), (1, 0), (2, 3), (3, 2)])
    stacks = lag_call(lag_own_kernel, place, spectra, inverse_count, old_stacks, lambda place: place[0])
    return merge(place, stacks, got, old_stacks)


def solution(mesh):
    return jax.shard_map(
        on_device,
        mesh=mesh,
        in_specs=(P(("rcv", "src"), None), P(), P(), P(None, "src", "rcv")),
        out_specs=P(None, "src", "rcv"),
        check_vma=False,
    )
```

```python
import functools
import math

import jax
import jax.numpy as jnp
import numpy as np
from jax import lax
from jax.experimental import pallas as pl
from jax.experimental.pallas import tpu as pltpu
from jax.sharding import PartitionSpec as P

WIN = 400
NFFT = 800
BINS = 401
LARGEST_LAG = 200
LAGS = 401
HALFBAND = 32
SUB = 32
EPSILON = 1e-06

PIECE = WIN // 4
PADDED = 112
DEPTH = 4 * PADDED
FREQ = 416
HALF = 128
SRC = 64
OWN = 32
SHIFTS = 208
PITCH = 72
SPITCH = 40
ROWS = 2 * SRC
XPITCH = ROWS + 8
BLOCK = 16
VMEM = 56 * 1024 * 1024


def split(table):
    high = table.astype(jnp.bfloat16)
    low = (table - high.astype(np.float32)).astype(jnp.bfloat16)
    return high, low


def forward_table():
    samples = np.arange(WIN)[None, :]
    bins = np.arange(BINS)[:, None]
    phases = (samples * bins % NFFT) * (2.0 * math.pi / NFFT)
    table = np.zeros((2, FREQ, 4, PADDED), np.float32)
    table[0, :BINS, :, :PIECE] = np.cos(phases).reshape(BINS, 4, PIECE)
    table[1, :BINS, :, :PIECE] = -np.sin(phases).reshape(BINS, 4, PIECE)
    high, low = split(table.reshape(2 * FREQ, DEPTH))
    sums = (high.astype(np.float64) + low.astype(np.float64)).sum(axis=1, keepdims=True)
    return high, low, np.broadcast_to((sums / WIN).astype(np.float32), (2 * FREQ, HALF)).copy()


def band_table():
    bins = np.arange(FREQ)
    inside = np.abs(bins[:, None] - bins[None, :]) <= HALFBAND
    inside &= (bins[:, None] < BINS) & (bins[None, :] < BINS)
    counts = np.maximum(inside.sum(axis=1, keepdims=True), 1)
    inverse = np.broadcast_to((1.0 / (2.0 * counts)).astype(np.float32), (FREQ, HALF)).copy()
    return inside.astype(jnp.bfloat16), inverse


def lag_tables():
    shifts = np.arange(LARGEST_LAG + 1)[:, None]
    bins = np.arange(BINS)[None, :]
    phases = (shifts * bins % NFFT) * (2.0 * math.pi / NFFT)
    weights = np.where((bins == 0) | (bins == NFFT // 2), 1.0, 2.0) / math.sqrt(NFFT)
    tables = np.zeros((2, SHIFTS, FREQ), np.float32)
    tables[0, : LARGEST_LAG + 1, :BINS] = weights * np.cos(phases)
    tables[1, : LARGEST_LAG + 1, :BINS] = -weights * np.sin(phases)
    return tables.astype(jnp.bfloat16)


def dot(a, b):
    return jnp.dot(a, b, preferred_element_type=jnp.float32)


def whiten_pair(x_ref, flag_ref, high_ref, low_ref, sums_ref, band_ref, inverse_ref, spec):
    x = jnp.concatenate([x_ref[0], x_ref[1]], axis=1)
    spec[...] = dot(high_ref[...], x) + dot(low_ref[...], x)
    total = spec[0:1, :]
    sums = sums_ref[...]
    sums = jnp.concatenate([sums, sums], axis=1)
    real = spec[:FREQ] - sums[:FREQ] * total
    imag = spec[FREQ:] - sums[FREQ:] * total
    power = real * real + imag * imag
    power_high = power.astype(jnp.bfloat16)
    power_low = (power - power_high.astype(jnp.float32)).astype(jnp.bfloat16)
    band = band_ref[...]
    smooth = dot(band, power_high) + dot(band, power_low)
    inverse = inverse_ref[...]
    inverse = jnp.concatenate([inverse, inverse], axis=1)
    flags = jnp.concatenate([flag_ref[0], flag_ref[1]], axis=1)
    scale = flags * lax.rsqrt(smooth * inverse + EPSILON)
    return real * scale, imag * scale


def whiten_sources_kernel(
    x_ref, flag_ref, high_ref, low_ref, sums_ref, band_ref, inverse_ref, out_ref, spec, held
):
    step = pl.program_id(0)
    real, imag = whiten_pair(x_ref, flag_ref, high_ref, low_ref, sums_ref, band_ref, inverse_ref, spec)
    for g in range(2):
        group = 2 * step + g
        first = pl.ds(group, FREQ, stride=SPITCH)
        second = pl.ds(SUB // 2 + group, FREQ, stride=SPITCH)
        own_real = real[:, g * HALF : (g + 1) * HALF]
        own_imag = imag[:, g * HALF : (g + 1) * HALF]
        held[0, first, :] = own_real
        held[0, second, :] = own_imag
        held[1, first, :] = -own_imag
        held[1, second, :] = own_real

    @pl.when(step == pl.num_programs(0) - 1)
    def _():
        low_lanes = lax.broadcasted_iota(jnp.int32, (SRC, HALF), 1) < HALF // 2

        @pl.loop(0, FREQ // 4)
        def _(quad):
            for part in range(2):
                rows = [
                    held[part, pl.ds(pl.multiple_of((4 * quad + i) * SPITCH, 8), SUB), :] for i in range(4)
                ]
                turned = jnp.concatenate(rows, axis=0).T
                first, second = turned[:SRC], turned[SRC:]
                pairs = (
                    jnp.where(low_lanes, first, pltpu.roll(second, HALF // 2, 1)),
                    jnp.where(low_lanes, pltpu.roll(first, HALF // 2, 1), second),
                )
                for i in range(2):
                    out_ref[2 * quad + i, part * SRC : (part + 1) * SRC] = pairs[i].astype(jnp.bfloat16)


def whiten_receivers_kernel(place_ref, x_ref, flag_ref, high_ref, low_ref, sums_ref, band_ref, inverse_ref, out_ref, spec, held):
    step = pl.program_id(0)
    real, imag = whiten_pair(x_ref, flag_ref, high_ref, low_ref, sums_ref, band_ref, inverse_ref, spec)
    for g in range(2):
        row = g * SUB + step
        held[pl.ds(row, FREQ, stride=PITCH), :] = real[:, g * HALF : (g + 1) * HALF]
        held[pl.ds(row + SUB // 2, FREQ, stride=PITCH), :] = imag[:, g * HALF : (g + 1) * HALF]

    @pl.when(step == pl.num_programs(0) - 1)
    def _():
        @pl.loop(0, FREQ // 8)
        def _(block):
            for i in range(8):
                f = block * 8 + i
                out_ref[f] = held[pl.ds(pl.multiple_of(f * PITCH, 8), 2 * SUB), :].astype(jnp.bfloat16)


def whole(shape):
    return pl.BlockSpec(shape, lambda *_: (0,) * len(shape))


def whiten_tables():
    high, low, sums = forward_table()
    return [jnp.asarray(table) for table in (high, low, sums, *band_table())]


def whiten_cost(groups):
    return pl.CostEstimate(
        flops=groups * 4 * 2 * FREQ * DEPTH * HALF, bytes_accessed=groups * DEPTH * HALF * 6, transcendentals=0
    )


def whiten_receivers(place, x, flags):
    tables = whiten_tables()
    return pl.pallas_call(
        whiten_receivers_kernel,
        grid_spec=pltpu.PrefetchScalarGridSpec(
            num_scalar_prefetch=1,
            grid=(SUB // 2,),
            in_specs=[
                pl.BlockSpec((2, DEPTH, HALF), lambda g, place: (lax.bitwise_xor(g, place[1]), 0, 0)),
                pl.BlockSpec((2, 1, HALF), lambda g, place: (g, 0, 0)),
            ]
            + [whole(table.shape) for table in tables],
            out_specs=whole((FREQ, 2 * SUB, HALF)),
            scratch_shapes=[
                pltpu.VMEM((2 * FREQ, 2 * HALF), jnp.float32),
                pltpu.VMEM((FREQ * PITCH, HALF), jnp.float32),
            ],
        ),
        out_shape=jax.ShapeDtypeStruct((FREQ, 2 * SUB, HALF), jnp.bfloat16),
        compiler_params=pltpu.CompilerParams(vmem_limit_bytes=VMEM),
        cost_estimate=whiten_cost(SUB),
    )(place, x, flags, *tables)


def whiten_sources(x, flags):
    tables = whiten_tables()
    return pl.pallas_call(
        whiten_sources_kernel,
        grid=(SUB // 4,),
        in_specs=[
            pl.BlockSpec((2, DEPTH, HALF), lambda g: (g, 0, 0)),
            pl.BlockSpec((2, 1, HALF), lambda g: (g, 0, 0)),
        ]
        + [whole(table.shape) for table in tables],
        out_specs=whole((FREQ // 2, ROWS, HALF)),
        out_shape=jax.ShapeDtypeStruct((FREQ // 2, ROWS, HALF), jnp.bfloat16),
        scratch_shapes=[
            pltpu.VMEM((2 * FREQ, 2 * HALF), jnp.float32),
            pltpu.VMEM((2, FREQ * SPITCH, HALF), jnp.float32),
        ],
        compiler_params=pltpu.CompilerParams(vmem_limit_bytes=VMEM),
        cost_estimate=whiten_cost(SUB // 2),
    )(x, flags, *tables)


def cross_kernel(left_ref, right_ref, out_ref, held):
    zeros = jnp.zeros((2 * SUB, HALF), jnp.bfloat16)
    for pair in range(BLOCK // 2):
        first = jnp.concatenate([right_ref[2 * pair], zeros], axis=1)
        second = jnp.concatenate([zeros, right_ref[2 * pair + 1]], axis=1)
        weights = jnp.concatenate([first[:SUB], second[:SUB], first[SUB:], second[SUB:]], axis=0)
        product = dot(left_ref[pair], weights)
        held[pl.ds(2 * pair * XPITCH, ROWS), :] = product[:, :HALF]
        held[pl.ds((2 * pair + 1) * XPITCH, ROWS), :] = product[:, HALF:]
    for row in range(ROWS):
        out_ref[row] = held[pl.ds(row, BLOCK, stride=XPITCH), :].astype(jnp.bfloat16)


def cross(left, right):
    return pl.pallas_call(
        cross_kernel,
        grid=(FREQ // BLOCK,),
        in_specs=[
            pl.BlockSpec((BLOCK // 2, ROWS, 4 * SUB), lambda f: (f, 0, 0)),
            pl.BlockSpec((BLOCK, 2 * SUB, HALF), lambda f: (f, 0, 0)),
        ],
        out_specs=pl.BlockSpec((ROWS, BLOCK, HALF), lambda f: (0, f, 0)),
        out_shape=jax.ShapeDtypeStruct((ROWS, FREQ, HALF), jnp.bfloat16),
        scratch_shapes=[pltpu.VMEM((BLOCK * XPITCH, HALF), jnp.float32)],
        compiler_params=pltpu.CompilerParams(vmem_limit_bytes=VMEM),
        cost_estimate=pl.CostEstimate(flops=FREQ * ROWS * 4 * SUB * 2 * HALF, bytes_accessed=30 << 20, transcendentals=0),
    )(left, right)


def lag_sums(real_ref, imag_ref, tables_ref, even, odd):
    for pair in range(BLOCK // 2):
        real = jnp.concatenate([real_ref[2 * pair], real_ref[2 * pair + 1]], axis=1)
        imag = jnp.concatenate([imag_ref[2 * pair], imag_ref[2 * pair + 1]], axis=1)
        cosine = dot(tables_ref[0], real)
        sine = dot(tables_ref[1], imag)
        for i in range(2):
            rows = pl.ds(2 * pair + i, SHIFTS, stride=BLOCK)
            even[rows, :] = cosine[:, i * HALF : (i + 1) * HALF]
            odd[rows, :] = sine[:, i * HALF : (i + 1) * HALF]


def shift_rows(m):
    return pl.ds(pl.multiple_of(m * BLOCK, BLOCK), BLOCK)


def lag_partner_kernel(place_ref, real_ref, imag_ref, tables_ref, count_ref, out_ref, even, odd):
    lag_sums(real_ref, imag_ref, tables_ref, even, odd)

    @pl.loop(0, LARGEST_LAG + 1, unroll=3)
    def _(m):
        e, o = even[shift_rows(m), :], odd[shift_rows(m), :]
        out_ref[LARGEST_LAG + m] = ((e + o) * count_ref[...]).astype(jnp.bfloat16)
        out_ref[LARGEST_LAG - m] = ((e - o) * count_ref[...]).astype(jnp.bfloat16)


def lag_own_kernel(place_ref, real_ref, imag_ref, tables_ref, count_ref, old_ref, out_ref, even, odd):
    lag_sums(real_ref, imag_ref, tables_ref, even, odd)

    @pl.loop(0, LARGEST_LAG + 1, unroll=3)
    def _(m):
        e, o = even[shift_rows(m), :], odd[shift_rows(m), :]
        above, below = LARGEST_LAG + m, LARGEST_LAG - m
        out_ref[above] = old_ref[above].astype(jnp.float32) + (e + o) * count_ref[...]
        out_ref[below] = old_ref[below].astype(jnp.float32) + (e - o) * count_ref[...]


def lag_call(kernel, place, spectra, inverse_count, old, half):
    steps = OWN // BLOCK
    tables = lag_tables()
    in_specs = [
        pl.BlockSpec((BLOCK, FREQ, HALF), lambda g, place: (half(place) * steps + g, 0, 0)),
        pl.BlockSpec((BLOCK, FREQ, HALF), lambda g, place: (SRC // BLOCK + half(place) * steps + g, 0, 0)),
        pl.BlockSpec(tables.shape, lambda g, place: (0, 0, 0)),
        pl.BlockSpec((BLOCK, HALF), lambda g, place: (half(place) * steps + g, 0)),
    ]
    operands = [spectra, spectra, jnp.asarray(tables), inverse_count]
    if old is None:
        out_shape = jax.ShapeDtypeStruct((LAGS, OWN, HALF), jnp.bfloat16)
        out_spec = pl.BlockSpec((LAGS, BLOCK, HALF), lambda g, place: (0, g, 0))
    else:
        in_specs.append(pl.BlockSpec((LAGS, BLOCK, HALF), lambda g, place: (0, g, place[0])))
        operands.append(old)
        out_shape = jax.ShapeDtypeStruct((LAGS, OWN, 2 * HALF), jnp.float32)
        out_spec = pl.BlockSpec((LAGS, BLOCK, HALF), lambda g, place: (0, g, place[0]))
    return pl.pallas_call(
        kernel,
        grid_spec=pltpu.PrefetchScalarGridSpec(
            num_scalar_prefetch=1,
            grid=(steps,),
            in_specs=in_specs,
            out_specs=out_spec,
            scratch_shapes=[pltpu.VMEM((SHIFTS * BLOCK, HALF), jnp.float32)] * 2,
        ),
        out_shape=out_shape,
        compiler_params=pltpu.CompilerParams(vmem_limit_bytes=VMEM),
        cost_estimate=pl.CostEstimate(flops=OWN * SHIFTS * FREQ * HALF * 4, bytes_accessed=16 << 20, transcendentals=0),
    )(place, *operands)


def merge_kernel(place_ref, held_ref, got_ref, old_ref, out_ref):
    out_ref[...] = old_ref[...].astype(jnp.float32) + got_ref[...].astype(jnp.float32)


def merge(place, stacks, got, old):
    rows = 58
    spec = pl.BlockSpec((rows, OWN, HALF), lambda l, place: (l, 0, 1 - place[0]))
    return pl.pallas_call(
        merge_kernel,
        grid_spec=pltpu.PrefetchScalarGridSpec(
            num_scalar_prefetch=1,
            grid=(pl.cdiv(LAGS, rows),),
            in_specs=[
                pl.BlockSpec(memory_space=pl.ANY),
                pl.BlockSpec((rows, OWN, HALF), lambda l, place: (l, 0, 0)),
                spec,
            ],
            out_specs=spec,
        ),
        out_shape=jax.ShapeDtypeStruct(stacks.shape, stacks.dtype),
        input_output_aliases={1: 0},
        compiler_params=pltpu.CompilerParams(vmem_limit_bytes=VMEM),
        cost_estimate=pl.CostEstimate(flops=LAGS * OWN * HALF, bytes_accessed=13 << 20, transcendentals=0),
    )(place, stacks, got, old)


def device(x, y, z_low, z_high, core):
    return ((x * 4 + y) * 2 + z_low) * 4 + z_high * 2 + core


def send(value, route):
    places = [(x, y, l, h, c) for x in range(4) for y in range(4) for l in range(2) for h in range(2) for c in range(2)]
    return lax.ppermute(value, ("rcv", "src"), [(device(*place), device(*route(*place))) for place in places])


def near_sources(record, z_low, z_high):
    near = record[:, : 2 * SRC]
    same = jnp.where(z_high == 0, near[:, :SRC], near[:, SRC:])
    other = jnp.where(z_high == 0, near[:, SRC:], near[:, :SRC])
    low = send(same, lambda x, y, l, h, c: (x, y, 1 - l, h, c))
    high = send(other, lambda x, y, l, h, c: (x, y, l, 1 - h, c))
    both = send(other, lambda x, y, l, h, c: (x, y, 1 - l, 1 - h, c))

    def windows(mine, theirs):
        return jnp.where(z_low == 0, jnp.concatenate([mine, theirs], 1), jnp.concatenate([theirs, mine], 1))

    mine, theirs = windows(same, low), windows(high, both)
    rows = jnp.where(z_high == 0, jnp.stack([mine, theirs]), jnp.stack([theirs, mine]))
    return jnp.pad(rows, ((0, 0), (0, PADDED - PIECE), (0, 0)))


def plane_sources(near):
    column = jnp.stack([near] + [send(near, lambda x, y, l, h, c, d=d: (x, y ^ d, l, h, c)) for d in (1, 2, 3)])
    plane = jnp.stack([column] + [send(column, lambda x, y, l, h, c, d=d: (x ^ d, y, l, h, c)) for d in (1, 2, 3)])
    return plane.reshape(SUB // 2, 2, PADDED, HALF)


def both_cores(plane, core):
    other = send(plane, lambda x, y, l, h, c: (x, y, l, h, 1 - c))
    rows = jnp.where(core == 0, jnp.stack([plane, other], axis=2), jnp.stack([other, plane], axis=2))
    return rows.reshape(SUB // 2, DEPTH, HALF)


def on_device(record, quality, keep_flags, old_stacks):
    row = lax.axis_index("rcv")
    col = lax.axis_index("src")
    core = lax.rem(col, 2)
    chip = lax.div(col, 2)
    z_low = lax.rem(row, 2)
    group = lax.div(row, 2)
    place = jnp.stack([core, group]).astype(jnp.int32)
    blocks = lax.axis_size("rcv")

    pieces = jnp.pad(record, ((0, PADDED - PIECE), (0, 0)))
    pieces = pieces.reshape(PADDED, blocks, 1, 2, HALF).transpose(1, 2, 3, 0, 4)
    pieces = jnp.broadcast_to(pieces, (blocks, 2, 2, PADDED, HALF)).reshape(4 * blocks, PADDED, HALF)
    plane = plane_sources(near_sources(record, z_low, chip))
    plane, pieces = lax.optimization_barrier((plane, pieces))
    receivers = lax.all_to_all(pieces, ("rcv", "src"), split_axis=0, concat_axis=0, tiled=True)
    sources = both_cores(plane, core)

    keep_all = keep_flags.astype(jnp.float32)
    flags = keep_all * quality.astype(jnp.float32)[None, :]
    first_receiver = row * 2 * HALF + core * HALF
    keep_src = lax.dynamic_slice_in_dim(keep_all, chip * SRC, SRC, 1)
    keep_rcv = lax.dynamic_slice_in_dim(keep_all, first_receiver, HALF, 1)
    inverse_count = 1.0 / jnp.maximum(dot(keep_src.T, keep_rcv), 1.0)
    order = lax.bitwise_xor(jnp.arange(SUB // 2, dtype=jnp.int32), group.astype(jnp.int32))
    flags_src = lax.dynamic_slice_in_dim(flags, chip * SRC, SRC, 1).reshape(SUB // 2, 1, 2 * SRC)[order]
    flags_rcv = lax.dynamic_slice_in_dim(flags, first_receiver, HALF, 1).reshape(SUB // 2, 2, HALF)[order]

    left = whiten_sources(sources, flags_src)
    right = whiten_receivers(place, receivers.reshape(SUB, DEPTH, HALF), flags_rcv.reshape(SUB, 1, HALF))
    spectra = cross(left, right)
    away = lag_call(lag_partner_kernel, place, spectra, inverse_count, None, lambda place: 1 - place[0])
    got = lax.ppermute(away, "src", [(0, 1), (1, 0), (2, 3), (3, 2)])
    stacks = lag_call(lag_own_kernel, place, spectra, inverse_count, old_stacks, lambda place: place[0])
    return merge(place, stacks, got, old_stacks)


def solution(mesh):
    return jax.shard_map(
        on_device,
        mesh=mesh,
        in_specs=(P(("rcv", "src"), None), P(), P(), P(None, "src", "rcv")),
        out_specs=P(None, "src", "rcv"),
        check_vma=False,
    )
```

```python
import functools
import math

import jax
import jax.numpy as jnp
import numpy as np
from jax import lax
from jax.experimental import pallas as pl
from jax.experimental.pallas import tpu as pltpu
from jax.sharding import PartitionSpec as P

WIN = 400
NFFT = 800
BINS = 401
LARGEST_LAG = 200
LAGS = 401
HALFBAND = 32
SUB = 32
EPSILON = 1e-06

PIECE = WIN // 4
PADDED = 112
DEPTH = 4 * PADDED
FREQ = 416
HALF = 128
SRC = 64
OWN = 32
SHIFTS = 208
PITCH = 72
SPITCH = 40
ROWS = 2 * SRC
XPITCH = ROWS + 8
BLOCK = 16
PAIRS = 4
VMEM = 56 * 1024 * 1024


def split(table):
    high = table.astype(jnp.bfloat16)
    low = (table - high.astype(np.float32)).astype(jnp.bfloat16)
    return high, low


def forward_table():
    samples = np.arange(WIN)[None, :]
    bins = np.arange(BINS)[:, None]
    phases = (samples * bins % NFFT) * (2.0 * math.pi / NFFT)
    table = np.zeros((2, FREQ, 4, PADDED), np.float32)
    table[0, :BINS, :, :PIECE] = np.cos(phases).reshape(BINS, 4, PIECE)
    table[1, :BINS, :, :PIECE] = -np.sin(phases).reshape(BINS, 4, PIECE)
    high, low = split(table.reshape(2 * FREQ, DEPTH))
    sums = (high.astype(np.float64) + low.astype(np.float64)).sum(axis=1, keepdims=True)
    sums = np.broadcast_to((sums / WIN).astype(np.float32), (2 * FREQ, HALF)).copy()
    return np.concatenate([high, low], axis=1), sums


def band_table():
    bins = np.arange(FREQ)
    inside = np.abs(bins[:, None] - bins[None, :]) <= HALFBAND
    inside &= (bins[:, None] < BINS) & (bins[None, :] < BINS)
    counts = np.maximum(inside.sum(axis=1, keepdims=True), 1)
    inverse = np.broadcast_to((1.0 / (2.0 * counts)).astype(np.float32), (FREQ, HALF)).copy()
    return np.concatenate([inside, inside], axis=1).astype(jnp.bfloat16), inverse


def lag_tables():
    shifts = np.arange(LARGEST_LAG + 1)[:, None]
    bins = np.arange(BINS)[None, :]
    phases = (shifts * bins % NFFT) * (2.0 * math.pi / NFFT)
    weights = np.where((bins == 0) | (bins == NFFT // 2), 1.0, 2.0) / math.sqrt(NFFT)
    tables = np.zeros((2, SHIFTS, FREQ), np.float32)
    tables[0, : LARGEST_LAG + 1, :BINS] = weights * np.cos(phases)
    tables[1, : LARGEST_LAG + 1, :BINS] = -weights * np.sin(phases)
    return tables.astype(jnp.bfloat16)


def dot(a, b):
    return jnp.dot(a, b, preferred_element_type=jnp.float32)


def clear_pad(samples):
    samples[...] = jnp.zeros(samples.shape, samples.dtype)


def whiten_pair(pieces, flags, samples, table_ref, sums_ref, band_ref, inverse_ref, spec):
    for g in range(2):
        for j in range(4):
            samples[pl.ds(j * PADDED, PIECE), g * HALF : (g + 1) * HALF] = pieces[g][j][...]
    x = samples[...]
    x = jnp.concatenate([x, x], axis=0)
    for i in range(4):
        rows = pl.ds(i * SHIFTS, SHIFTS)
        spec[rows, :] = dot(table_ref[rows, :], x)
    total = spec[0:1, :]
    sums = sums_ref[...]
    sums = jnp.concatenate([sums, sums], axis=1)
    real = spec[:FREQ] - sums[:FREQ] * total
    imag = spec[FREQ:] - sums[FREQ:] * total
    power = real * real + imag * imag
    power_high = power.astype(jnp.bfloat16)
    power_low = (power - power_high.astype(jnp.float32)).astype(jnp.bfloat16)
    power = jnp.concatenate([power_high, power_low], axis=0)
    smooth = jnp.concatenate([dot(band_ref[:SHIFTS], power), dot(band_ref[SHIFTS:], power)], axis=0)
    inverse = inverse_ref[...]
    inverse = jnp.concatenate([inverse, inverse], axis=1)
    scale = flags * lax.rsqrt(smooth * inverse + EPSILON)
    return real * scale, imag * scale


def whiten_sources_kernel(
    x_ref, flag_ref, table_ref, sums_ref, band_ref, inverse_ref, out_ref, samples, spec, held
):
    step = pl.program_id(0)

    @pl.when(step == 0)
    def _():
        clear_pad(samples)

    pieces = [[x_ref.at[g, j] for j in range(4)] for g in range(2)]
    flags = jnp.concatenate([flag_ref[0], flag_ref[1]], axis=1)
    real, imag = whiten_pair(pieces, flags, samples, table_ref, sums_ref, band_ref, inverse_ref, spec)
    for g in range(2):
        group = 2 * step + g
        first = pl.ds(group, FREQ, stride=SPITCH)
        second = pl.ds(SUB // 2 + group, FREQ, stride=SPITCH)
        own_real = real[:, g * HALF : (g + 1) * HALF]
        own_imag = imag[:, g * HALF : (g + 1) * HALF]
        held[0, first, :] = own_real
        held[0, second, :] = own_imag
        held[1, first, :] = -own_imag
        held[1, second, :] = own_real

    @pl.when(step == pl.num_programs(0) - 1)
    def _():
        low_lanes = lax.broadcasted_iota(jnp.int32, (SRC, HALF), 1) < HALF // 2

        @pl.loop(0, FREQ // 4)
        def _(quad):
            for part in range(2):
                rows = [
                    held[part, pl.ds(pl.multiple_of((4 * quad + i) * SPITCH, 8), SUB), :] for i in range(4)
                ]
                turned = jnp.concatenate(rows, axis=0).T
                first, second = turned[:SRC], turned[SRC:]
                pairs = (
                    jnp.where(low_lanes, first, pltpu.roll(second, HALF // 2, 1)),
                    jnp.where(low_lanes, pltpu.roll(first, HALF // 2, 1), second),
                )
                for i in range(2):
                    out_ref[2 * quad + i, part * SRC : (part + 1) * SRC] = pairs[i].astype(jnp.bfloat16)


def whole(shape):
    return pl.BlockSpec(shape, lambda *_: (0,) * len(shape))


def whiten_tables():
    return [jnp.asarray(table) for table in (*forward_table(), *band_table())]


def whiten_cost(groups):
    return pl.CostEstimate(
        flops=groups * 4 * 2 * FREQ * DEPTH * HALF, bytes_accessed=groups * DEPTH * HALF * 6, transcendentals=0
    )


def whiten_sources(x, flags):
    tables = whiten_tables()
    return pl.pallas_call(
        whiten_sources_kernel,
        grid=(SUB // 4,),
        in_specs=[
            pl.BlockSpec((2, 4, PIECE, HALF), lambda g: (g, 0, 0, 0)),
            pl.BlockSpec((2, 1, HALF), lambda g: (g, 0, 0)),
        ]
        + [whole(table.shape) for table in tables],
        out_specs=whole((FREQ // 2, ROWS, HALF)),
        out_shape=jax.ShapeDtypeStruct((FREQ // 2, ROWS, HALF), jnp.bfloat16),
        scratch_shapes=[
            pltpu.VMEM((DEPTH, 2 * HALF), jnp.bfloat16),
            pltpu.VMEM((2 * FREQ, 2 * HALF), jnp.float32),
            pltpu.VMEM((2, FREQ * SPITCH, HALF), jnp.float32),
        ],
        compiler_params=pltpu.CompilerParams(vmem_limit_bytes=VMEM),
        cost_estimate=whiten_cost(SUB // 2),
    )(x, flags, *tables)


def lag_sums(real_ref, imag_ref, tables_ref, even, odd):
    for pair in range(BLOCK // 2):
        real = jnp.concatenate([real_ref[2 * pair], real_ref[2 * pair + 1]], axis=1)
        imag = jnp.concatenate([imag_ref[2 * pair], imag_ref[2 * pair + 1]], axis=1)
        cosine = dot(tables_ref[0], real)
        sine = dot(tables_ref[1], imag)
        for i in range(2):
            rows = pl.ds(2 * pair + i, SHIFTS, stride=BLOCK)
            even[rows, :] = cosine[:, i * HALF : (i + 1) * HALF]
            odd[rows, :] = sine[:, i * HALF : (i + 1) * HALF]


def shift_rows(m):
    return pl.ds(pl.multiple_of(m * BLOCK, BLOCK), BLOCK)


def stack_kernel(
    place_ref,
    x_ref,
    flag_ref,
    table_ref,
    sums_ref,
    band_ref,
    inverse_ref,
    tables_ref,
    count_ref,
    left_hbm,
    away_ref,
    own_hbm,
    samples,
    spec,
    held,
    left_ref,
    spectra,
    products,
    even,
    odd,
    sems,
):
    step = pl.program_id(0)
    core = place_ref[0]
    inner = lax.rem(place_ref[1], PAIRS)
    left_copy = pltpu.make_async_copy(left_hbm, left_ref, sems.at[0])

    @pl.when(step == 0)
    def _():
        left_copy.start()
        clear_pad(samples)

    for p in range(PAIRS):
        source = lax.bitwise_xor(p, inner)
        pieces = [[x_ref.at[source, g, j] for j in range(4)] for g in range(2)]
        flags = jnp.concatenate([flag_ref[p, 0], flag_ref[p, 1]], axis=1)
        real, imag = whiten_pair(
            pieces, flags, samples.at[p % 2], table_ref, sums_ref, band_ref, inverse_ref, spec.at[p % 2]
        )
        for g in range(2):
            row = g * SUB + step * PAIRS + p
            held[pl.ds(row, FREQ, stride=PITCH), :] = real[:, g * HALF : (g + 1) * HALF]
            held[pl.ds(row + SUB // 2, FREQ, stride=PITCH), :] = imag[:, g * HALF : (g + 1) * HALF]

    @pl.when(step == pl.num_programs(0) - 1)
    def _():
        left_copy.wait()
        zeros = jnp.zeros((2 * SUB, HALF), jnp.bfloat16)

        def receivers(f):
            return held[pl.ds(pl.multiple_of(f * PITCH, 8), 2 * SUB), :].astype(jnp.bfloat16)

        @pl.loop(0, FREQ // (2 * BLOCK))
        def _(outer):
            for side in range(2):
                block = 2 * outer + side
                for pair in range(BLOCK // 2):
                    f = block * BLOCK + 2 * pair
                    first = jnp.concatenate([receivers(f), zeros], axis=1)
                    second = jnp.concatenate([zeros, receivers(f + 1)], axis=1)
                    weights = jnp.concatenate([first[:SUB], second[:SUB], first[SUB:], second[SUB:]], axis=0)
                    product = dot(left_ref[block * (BLOCK // 2) + pair], weights)
                    products[side, pl.ds(2 * pair * XPITCH, ROWS), :] = product[:, :HALF]
                    products[side, pl.ds((2 * pair + 1) * XPITCH, ROWS), :] = product[:, HALF:]
                bins = pl.ds(pl.multiple_of(block * BLOCK, BLOCK), BLOCK)
                for row in range(ROWS):
                    spectra[row, bins, :] = products[side, pl.ds(row, BLOCK, stride=XPITCH), :].astype(jnp.bfloat16)

        copies = [
            pltpu.make_async_copy(
                spectra.at[pl.ds(part * SRC + core * OWN, OWN)], own_hbm.at[pl.ds(part * OWN, OWN)], sems.at[1 + part]
            )
            for part in range(2)
        ]
        for copy in copies:
            copy.start()
        for g in range(OWN // BLOCK):
            first = (1 - core) * OWN + g * BLOCK
            lag_sums(
                spectra.at[pl.ds(first, BLOCK)], spectra.at[pl.ds(SRC + first, BLOCK)], tables_ref, even, odd
            )
            count = count_ref[pl.ds(pl.multiple_of(first, BLOCK), BLOCK), :]

            @pl.loop(0, LARGEST_LAG + 1, unroll=3)
            def _(m):
                e, o = even[shift_rows(m), :], odd[shift_rows(m), :]
                sources = pl.ds(g * BLOCK, BLOCK)
                away_ref[LARGEST_LAG + m, sources, :] = ((e + o) * count).astype(jnp.bfloat16)
                away_ref[LARGEST_LAG - m, sources, :] = ((e - o) * count).astype(jnp.bfloat16)

        for copy in copies:
            copy.wait()


def stack_partner(place, x, flags, left, inverse_count):
    tables = whiten_tables() + [jnp.asarray(lag_tables()), inverse_count]
    return pl.pallas_call(
        stack_kernel,
        grid_spec=pltpu.PrefetchScalarGridSpec(
            num_scalar_prefetch=1,
            grid=(SUB // 2 // PAIRS,),
            in_specs=[
                pl.BlockSpec(
                    (None, PAIRS, 2, 4, PIECE, HALF),
                    lambda g, place: (lax.bitwise_xor(g, lax.div(place[1], PAIRS)), 0, 0, 0, 0, 0),
                ),
                pl.BlockSpec((PAIRS, 2, 1, HALF), lambda g, place: (g, 0, 0, 0)),
            ]
            + [whole(table.shape) for table in tables]
            + [pl.BlockSpec(memory_space=pl.ANY)],
            out_specs=[whole((LAGS, OWN, HALF)), pl.BlockSpec(memory_space=pl.ANY)],
            scratch_shapes=[
                pltpu.VMEM((2, DEPTH, 2 * HALF), jnp.bfloat16),
                pltpu.VMEM((2, 2 * FREQ, 2 * HALF), jnp.float32),
                pltpu.VMEM((FREQ * PITCH, HALF), jnp.float32),
                pltpu.VMEM(left.shape, left.dtype),
                pltpu.VMEM((ROWS, FREQ, HALF), jnp.bfloat16),
                pltpu.VMEM((2, BLOCK * XPITCH, HALF), jnp.float32),
                pltpu.VMEM((SHIFTS * BLOCK, HALF), jnp.float32),
                pltpu.VMEM((SHIFTS * BLOCK, HALF), jnp.float32),
                pltpu.SemaphoreType.DMA((3,)),
            ],
        ),
        out_shape=[
            jax.ShapeDtypeStruct((LAGS, OWN, HALF), jnp.bfloat16),
            jax.ShapeDtypeStruct((2 * OWN, FREQ, HALF), jnp.bfloat16),
        ],
        compiler_params=pltpu.CompilerParams(vmem_limit_bytes=VMEM),
        cost_estimate=pl.CostEstimate(flops=30 * 10**9, bytes_accessed=24 << 20, transcendentals=0),
    )(place, x, flags, *tables, left)


def lag_own_kernel(place_ref, real_ref, imag_ref, tables_ref, count_ref, old_ref, out_ref, even, odd):
    lag_sums(real_ref, imag_ref, tables_ref, even, odd)

    @pl.loop(0, LARGEST_LAG + 1, unroll=8)
    def _(m):
        e, o = even[shift_rows(m), :], odd[shift_rows(m), :]
        above, below = LARGEST_LAG + m, LARGEST_LAG - m
        out_ref[above] = old_ref[above].astype(jnp.float32) + (e + o) * count_ref[...]
        out_ref[below] = old_ref[below].astype(jnp.float32) + (e - o) * count_ref[...]


def stack_own(place, spectra, inverse_count, old):
    steps = OWN // BLOCK
    tables = lag_tables()
    return pl.pallas_call(
        lag_own_kernel,
        grid_spec=pltpu.PrefetchScalarGridSpec(
            num_scalar_prefetch=1,
            grid=(steps,),
            in_specs=[
                pl.BlockSpec((BLOCK, FREQ, HALF), lambda g, place: (g, 0, 0)),
                pl.BlockSpec((BLOCK, FREQ, HALF), lambda g, place: (steps + g, 0, 0)),
                whole(tables.shape),
                pl.BlockSpec((BLOCK, HALF), lambda g, place: (place[0] * steps + g, 0)),
                pl.BlockSpec((LAGS, BLOCK, HALF), lambda g, place: (0, g, place[0])),
            ],
            out_specs=pl.BlockSpec((LAGS, BLOCK, HALF), lambda g, place: (0, g, place[0])),
            scratch_shapes=[pltpu.VMEM((SHIFTS * BLOCK, HALF), jnp.float32)] * 2,
        ),
        out_shape=jax.ShapeDtypeStruct((LAGS, OWN, 2 * HALF), jnp.float32),
        compiler_params=pltpu.CompilerParams(vmem_limit_bytes=VMEM),
        cost_estimate=pl.CostEstimate(flops=OWN * SHIFTS * FREQ * HALF * 4, bytes_accessed=16 << 20, transcendentals=0),
    )(place, spectra, spectra, jnp.asarray(tables), inverse_count, old)


def merge_kernel(place_ref, held_ref, got_ref, old_ref, out_ref):
    out_ref[...] = old_ref[...].astype(jnp.float32) + got_ref[...].astype(jnp.float32)


def merge(place, stacks, got, old):
    rows = 201
    spec = pl.BlockSpec((rows, OWN, HALF), lambda l, place: (l, 0, 1 - place[0]))
    return pl.pallas_call(
        merge_kernel,
        grid_spec=pltpu.PrefetchScalarGridSpec(
            num_scalar_prefetch=1,
            grid=(pl.cdiv(LAGS, rows),),
            in_specs=[
                pl.BlockSpec(memory_space=pl.ANY),
                pl.BlockSpec((rows, OWN, HALF), lambda l, place: (l, 0, 0)),
                spec,
            ],
            out_specs=spec,
        ),
        out_shape=jax.ShapeDtypeStruct(stacks.shape, stacks.dtype),
        input_output_aliases={1: 0},
        compiler_params=pltpu.CompilerParams(vmem_limit_bytes=VMEM),
        cost_estimate=pl.CostEstimate(flops=LAGS * OWN * HALF, bytes_accessed=13 << 20, transcendentals=0),
    )(place, stacks, got, old)


def outgoing_kernel(record_ref, out_ref):
    for i in range(out_ref.shape[0]):
        for core in range(2):
            column = (2 * i + core) * HALF
            piece = record_ref[:, column : column + HALF]
            for chip in range(2):
                out_ref[i, chip, core] = piece


def outgoing(record):
    blocks = record.shape[1] // (2 * HALF)
    steps = 4
    pieces = pl.pallas_call(
        outgoing_kernel,
        grid=(steps,),
        in_specs=[pl.BlockSpec((PIECE, record.shape[1] // steps), lambda i: (0, i))],
        out_specs=pl.BlockSpec((blocks // steps, 2, 2, PIECE, HALF), lambda i: (i, 0, 0, 0, 0)),
        out_shape=jax.ShapeDtypeStruct((blocks, 2, 2, PIECE, HALF), record.dtype),
        compiler_params=pltpu.CompilerParams(vmem_limit_bytes=VMEM),
        cost_estimate=pl.CostEstimate(flops=0, bytes_accessed=5 << 20, transcendentals=0),
    )(record)
    return pieces.reshape(4 * blocks, PIECE, HALF)


def device(x, y, z_low, z_high, core):
    return ((x * 4 + y) * 2 + z_low) * 4 + z_high * 2 + core


def send(value, route):
    places = [(x, y, l, h, c) for x in range(4) for y in range(4) for l in range(2) for h in range(2) for c in range(2)]
    return lax.ppermute(value, ("rcv", "src"), [(device(*place), device(*route(*place))) for place in places])


def near_sources(record, z_low, z_high):
    near = record[:, : 2 * SRC]
    same = jnp.where(z_high == 0, near[:, :SRC], near[:, SRC:])
    other = jnp.where(z_high == 0, near[:, SRC:], near[:, :SRC])
    low = send(same, lambda x, y, l, h, c: (x, y, 1 - l, h, c))
    high = send(other, lambda x, y, l, h, c: (x, y, l, 1 - h, c))
    both = send(other, lambda x, y, l, h, c: (x, y, 1 - l, 1 - h, c))

    def windows(mine, theirs):
        return jnp.where(z_low == 0, jnp.concatenate([mine, theirs], 1), jnp.concatenate([theirs, mine], 1))

    mine, theirs = windows(same, low), windows(high, both)
    return jnp.where(z_high == 0, jnp.stack([mine, theirs]), jnp.stack([theirs, mine]))


def plane_sources(near):
    column = jnp.stack([near] + [send(near, lambda x, y, l, h, c, d=d: (x, y ^ d, l, h, c)) for d in (1, 2, 3)])
    plane = jnp.stack([column] + [send(column, lambda x, y, l, h, c, d=d: (x ^ d, y, l, h, c)) for d in (1, 2, 3)])
    return plane.reshape(SUB // 2, 2, PIECE, HALF)


def both_cores(plane, core):
    other = send(plane, lambda x, y, l, h, c: (x, y, l, h, 1 - c))
    rows = jnp.where(core == 0, jnp.stack([plane, other], axis=2), jnp.stack([other, plane], axis=2))
    return rows.reshape(SUB // 2, 4, PIECE, HALF)


def on_device(record, quality, keep_flags, old_stacks):
    row = lax.axis_index("rcv")
    col = lax.axis_index("src")
    core = lax.rem(col, 2)
    chip = lax.div(col, 2)
    z_low = lax.rem(row, 2)
    group = lax.div(row, 2)
    place = jnp.stack([core, group]).astype(jnp.int32)

    pieces = outgoing(record)
    plane = plane_sources(near_sources(record, z_low, chip))
    plane, pieces = lax.optimization_barrier((plane, pieces))
    receivers = lax.all_to_all(pieces, ("rcv", "src"), split_axis=0, concat_axis=0, tiled=True)
    sources = both_cores(plane, core)

    keep_all = keep_flags.astype(jnp.float32)
    flags = keep_all * quality.astype(jnp.float32)[None, :]
    first_receiver = row * 2 * HALF + core * HALF
    keep_src = lax.dynamic_slice_in_dim(keep_all, chip * SRC, SRC, 1)
    keep_rcv = lax.dynamic_slice_in_dim(keep_all, first_receiver, HALF, 1)
    inverse_count = 1.0 / jnp.maximum(dot(keep_src.T, keep_rcv), 1.0)
    order = lax.bitwise_xor(jnp.arange(SUB // 2, dtype=jnp.int32), group.astype(jnp.int32))
    flags_src = lax.dynamic_slice_in_dim(flags, chip * SRC, SRC, 1).reshape(SUB // 2, 1, 2 * SRC)[order]
    flags_rcv = lax.dynamic_slice_in_dim(flags, first_receiver, HALF, 1).reshape(SUB // 2, 2, HALF)[order]

    left = whiten_sources(sources, flags_src)
    receivers = receivers.reshape(SUB // 2 // PAIRS, PAIRS, 2, 4, PIECE, HALF)
    flags_rcv = flags_rcv.reshape(SUB // 2, 2, 1, HALF)
    away, spectra = stack_partner(place, receivers, flags_rcv, left, inverse_count)
    got = lax.ppermute(away, "src", [(0, 1), (1, 0), (2, 3), (3, 2)])
    stacks = stack_own(place, spectra, inverse_count, old_stacks)
    return merge(place, stacks, got, old_stacks)


def solution(mesh):
    return jax.shard_map(
        on_device,
        mesh=mesh,
        in_specs=(P(("rcv", "src"), None), P(), P(), P(None, "src", "rcv")),
        out_specs=P(None, "src", "rcv"),
        check_vma=False,
    )
```

```python
import functools
import math

import jax
import jax.numpy as jnp
import numpy as np
from jax import lax
from jax.experimental import pallas as pl
from jax.experimental.pallas import tpu as pltpu
from jax.sharding import PartitionSpec as P

WIN = 400
NFFT = 800
BINS = 401
LARGEST_LAG = 200
LAGS = 401
HALFBAND = 32
SUB = 32
EPSILON = 1e-06

PIECE = WIN // 4
PADDED = 112
DEPTH = 4 * PADDED
FREQ = 416
HALF = 128
SRC = 64
OWN = 32
REACH = 256
SHIFTS = 208
PITCH = 72
SPITCH = 40
ROWS = 2 * SRC
XPITCH = ROWS + 8
BLOCK = 16
PAIRS = 4
VMEM = 56 * 1024 * 1024
ADD_VMEM = 62 * 1024 * 1024


def split(table):
    high = table.astype(jnp.bfloat16)
    low = (table - high.astype(np.float32)).astype(jnp.bfloat16)
    return high, low


def forward_table():
    samples = np.arange(WIN)[None, :]
    bins = np.arange(BINS)[:, None]
    phases = (samples * bins % NFFT) * (2.0 * math.pi / NFFT)
    table = np.zeros((2, FREQ, 4, PADDED), np.float32)
    table[0, :BINS, :, :PIECE] = np.cos(phases).reshape(BINS, 4, PIECE)
    table[1, :BINS, :, :PIECE] = -np.sin(phases).reshape(BINS, 4, PIECE)
    high, low = split(table.reshape(2 * FREQ, DEPTH))
    sums = (high.astype(np.float64) + low.astype(np.float64)).sum(axis=1, keepdims=True)
    sums = np.broadcast_to((sums / WIN).astype(np.float32), (2 * FREQ, HALF)).copy()
    return np.concatenate([high, low], axis=1), sums


def band_table():
    bins = np.arange(FREQ)
    inside = np.abs(bins[:, None] - bins[None, :]) <= HALFBAND
    inside &= (bins[:, None] < BINS) & (bins[None, :] < BINS)
    counts = np.maximum(inside.sum(axis=1, keepdims=True), 1)
    inverse = np.broadcast_to((1.0 / (2.0 * counts)).astype(np.float32), (FREQ, HALF)).copy()
    halves = np.stack([inside[:SHIFTS, :REACH], inside[SHIFTS:, FREQ - REACH :]])
    assert halves.sum() == inside.sum()
    return np.concatenate([halves, halves], axis=2).astype(jnp.bfloat16), inverse


def lag_tables():
    shifts = np.arange(LARGEST_LAG + 1)[:, None]
    bins = np.arange(BINS)[None, :]
    phases = (shifts * bins % NFFT) * (2.0 * math.pi / NFFT)
    weights = np.where((bins == 0) | (bins == NFFT // 2), 1.0, 2.0) / math.sqrt(NFFT)
    tables = np.zeros((2, SHIFTS, FREQ), np.float32)
    tables[0, : LARGEST_LAG + 1, :BINS] = weights * np.cos(phases)
    tables[1, : LARGEST_LAG + 1, :BINS] = -weights * np.sin(phases)
    return tables.astype(jnp.bfloat16)


def dot(a, b):
    return jnp.dot(a, b, preferred_element_type=jnp.float32)


def clear_pad(samples):
    samples[...] = jnp.zeros(samples.shape, samples.dtype)


def whiten_pair(pieces, flags, samples, table_ref, sums_ref, band_ref, inverse_ref, spec):
    for g in range(2):
        for j in range(4):
            samples[pl.ds(j * PADDED, PIECE), g * HALF : (g + 1) * HALF] = pieces[g][j][...]
    x = samples[...]
    x = jnp.concatenate([x, x], axis=0)
    for i in range(4):
        rows = pl.ds(i * SHIFTS, SHIFTS)
        spec[rows, :] = dot(table_ref[rows, :], x)
    total = spec[0:1, :]
    sums = sums_ref[...]
    sums = jnp.concatenate([sums, sums], axis=1)
    real = spec[:FREQ] - sums[:FREQ] * total
    imag = spec[FREQ:] - sums[FREQ:] * total
    power = real * real + imag * imag
    power_high = power.astype(jnp.bfloat16)
    power_low = (power - power_high.astype(jnp.float32)).astype(jnp.bfloat16)
    smooth = jnp.concatenate(
        [
            dot(band_ref[i], jnp.concatenate([part[first : first + REACH] for part in (power_high, power_low)], axis=0))
            for i, first in enumerate((0, FREQ - REACH))
        ],
        axis=0,
    )
    inverse = inverse_ref[...]
    inverse = jnp.concatenate([inverse, inverse], axis=1)
    scale = flags * lax.rsqrt(smooth * inverse + EPSILON)
    return real * scale, imag * scale


def whiten_sources_kernel(
    x_ref, flag_ref, table_ref, sums_ref, band_ref, inverse_ref, out_ref, samples, spec, held
):
    step = pl.program_id(0)

    @pl.when(step == 0)
    def _():
        clear_pad(samples)

    pieces = [[x_ref.at[g, j] for j in range(4)] for g in range(2)]
    flags = jnp.concatenate([flag_ref[0], flag_ref[1]], axis=1)
    real, imag = whiten_pair(pieces, flags, samples, table_ref, sums_ref, band_ref, inverse_ref, spec)
    for g in range(2):
        group = 2 * step + g
        first = pl.ds(group, FREQ, stride=SPITCH)
        second = pl.ds(SUB // 2 + group, FREQ, stride=SPITCH)
        own_real = real[:, g * HALF : (g + 1) * HALF]
        own_imag = imag[:, g * HALF : (g + 1) * HALF]
        held[0, first, :] = own_real
        held[0, second, :] = own_imag
        held[1, first, :] = -own_imag
        held[1, second, :] = own_real

    @pl.when(step == pl.num_programs(0) - 1)
    def _():
        low_lanes = lax.broadcasted_iota(jnp.int32, (SRC, HALF), 1) < HALF // 2

        @pl.loop(0, FREQ // 4)
        def _(quad):
            for part in range(2):
                rows = [
                    held[part, pl.ds(pl.multiple_of((4 * quad + i) * SPITCH, 8), SUB), :] for i in range(4)
                ]
                turned = jnp.concatenate(rows, axis=0).T
                first, second = turned[:SRC], turned[SRC:]
                pairs = (
                    jnp.where(low_lanes, first, pltpu.roll(second, HALF // 2, 1)),
                    jnp.where(low_lanes, pltpu.roll(first, HALF // 2, 1), second),
                )
                for i in range(2):
                    out_ref[2 * quad + i, part * SRC : (part + 1) * SRC] = pairs[i].astype(jnp.bfloat16)


def whole(shape):
    return pl.BlockSpec(shape, lambda *_: (0,) * len(shape))


def whiten_tables():
    return [jnp.asarray(table) for table in (*forward_table(), *band_table())]


def whiten_cost(groups):
    return pl.CostEstimate(
        flops=groups * 4 * 2 * FREQ * DEPTH * HALF, bytes_accessed=groups * DEPTH * HALF * 6, transcendentals=0
    )


def whiten_sources(x, flags):
    tables = whiten_tables()
    return pl.pallas_call(
        whiten_sources_kernel,
        grid=(SUB // 4,),
        in_specs=[
            pl.BlockSpec((2, 4, PIECE, HALF), lambda g: (g, 0, 0, 0)),
            pl.BlockSpec((2, 1, HALF), lambda g: (g, 0, 0)),
        ]
        + [whole(table.shape) for table in tables],
        out_specs=whole((FREQ // 2, ROWS, HALF)),
        out_shape=jax.ShapeDtypeStruct((FREQ // 2, ROWS, HALF), jnp.bfloat16),
        scratch_shapes=[
            pltpu.VMEM((DEPTH, 2 * HALF), jnp.bfloat16),
            pltpu.VMEM((2 * FREQ, 2 * HALF), jnp.float32),
            pltpu.VMEM((2, FREQ * SPITCH, HALF), jnp.float32),
        ],
        compiler_params=pltpu.CompilerParams(vmem_limit_bytes=VMEM),
        cost_estimate=whiten_cost(SUB // 2),
    )(x, flags, *tables)


def lag_sums(real_ref, imag_ref, tables_ref, even, odd):
    for pair in range(BLOCK // 2):
        real = jnp.concatenate([real_ref[2 * pair], real_ref[2 * pair + 1]], axis=1)
        imag = jnp.concatenate([imag_ref[2 * pair], imag_ref[2 * pair + 1]], axis=1)
        cosine = dot(tables_ref[0], real)
        sine = dot(tables_ref[1], imag)
        for i in range(2):
            rows = pl.ds(2 * pair + i, SHIFTS, stride=BLOCK)
            even[rows, :] = cosine[:, i * HALF : (i + 1) * HALF]
            odd[rows, :] = sine[:, i * HALF : (i + 1) * HALF]


def shift_rows(m):
    return pl.ds(pl.multiple_of(m * BLOCK, BLOCK), BLOCK)


def stack_kernel(
    place_ref,
    x_ref,
    flag_ref,
    table_ref,
    sums_ref,
    band_ref,
    inverse_ref,
    tables_ref,
    count_ref,
    left_hbm,
    away_ref,
    mine_ref,
    samples,
    spec,
    held,
    left_ref,
    spectra,
    products,
    even,
    odd,
    sem,
):
    step = pl.program_id(0)
    core = place_ref[0]
    inner = lax.rem(place_ref[1], PAIRS)
    left_copy = pltpu.make_async_copy(left_hbm, left_ref, sem)

    @pl.when(step == 0)
    def _():
        left_copy.start()
        clear_pad(samples)

    for p in range(PAIRS):
        source = lax.bitwise_xor(p, inner)
        pieces = [[x_ref.at[source, g, j] for j in range(4)] for g in range(2)]
        flags = jnp.concatenate([flag_ref[p, 0], flag_ref[p, 1]], axis=1)
        real, imag = whiten_pair(
            pieces, flags, samples.at[p % 2], table_ref, sums_ref, band_ref, inverse_ref, spec.at[p % 2]
        )
        for g in range(2):
            row = g * SUB + step * PAIRS + p
            held[pl.ds(row, FREQ, stride=PITCH), :] = real[:, g * HALF : (g + 1) * HALF]
            held[pl.ds(row + SUB // 2, FREQ, stride=PITCH), :] = imag[:, g * HALF : (g + 1) * HALF]

    @pl.when(step == pl.num_programs(0) - 1)
    def _():
        left_copy.wait()
        zeros = jnp.zeros((2 * SUB, HALF), jnp.bfloat16)

        def receivers(f):
            return held[pl.ds(pl.multiple_of(f * PITCH, 8), 2 * SUB), :].astype(jnp.bfloat16)

        @pl.loop(0, FREQ // (2 * BLOCK))
        def _(outer):
            for side in range(2):
                block = 2 * outer + side
                for pair in range(BLOCK // 2):
                    f = block * BLOCK + 2 * pair
                    first = jnp.concatenate([receivers(f), zeros], axis=1)
                    second = jnp.concatenate([zeros, receivers(f + 1)], axis=1)
                    weights = jnp.concatenate([first[:SUB], second[:SUB], first[SUB:], second[SUB:]], axis=0)
                    product = dot(left_ref[block * (BLOCK // 2) + pair], weights)
                    products[side, pl.ds(2 * pair * XPITCH, ROWS), :] = product[:, :HALF]
                    products[side, pl.ds((2 * pair + 1) * XPITCH, ROWS), :] = product[:, HALF:]
                bins = pl.ds(pl.multiple_of(block * BLOCK, BLOCK), BLOCK)
                for row in range(ROWS):
                    spectra[row, bins, :] = products[side, pl.ds(row, BLOCK, stride=XPITCH), :].astype(jnp.bfloat16)

        for half, out_ref in ((1 - core, away_ref), (core, mine_ref)):
            for g in range(OWN // BLOCK):
                first = half * OWN + g * BLOCK
                lag_sums(
                    spectra.at[pl.ds(first, BLOCK)], spectra.at[pl.ds(SRC + first, BLOCK)], tables_ref, even, odd
                )
                count = count_ref[pl.ds(pl.multiple_of(first, BLOCK), BLOCK), :]

                @pl.loop(0, LARGEST_LAG + 1, unroll=8)
                def _(m):
                    e, o = even[shift_rows(m), :], odd[shift_rows(m), :]
                    sources = pl.ds(g * BLOCK, BLOCK)
                    out_ref[LARGEST_LAG + m, sources, :] = ((e + o) * count).astype(jnp.bfloat16)
                    out_ref[LARGEST_LAG - m, sources, :] = ((e - o) * count).astype(jnp.bfloat16)


def stack_halves(place, x, flags, left, inverse_count):
    tables = whiten_tables() + [jnp.asarray(lag_tables()), inverse_count]
    return pl.pallas_call(
        stack_kernel,
        grid_spec=pltpu.PrefetchScalarGridSpec(
            num_scalar_prefetch=1,
            grid=(SUB // 2 // PAIRS,),
            in_specs=[
                pl.BlockSpec(
                    (None, PAIRS, 2, 4, PIECE, HALF),
                    lambda g, place: (lax.bitwise_xor(g, lax.div(place[1], PAIRS)), 0, 0, 0, 0, 0),
                ),
                pl.BlockSpec((PAIRS, 2, 1, HALF), lambda g, place: (g, 0, 0, 0)),
            ]
            + [whole(table.shape) for table in tables]
            + [pl.BlockSpec(memory_space=pl.ANY)],
            out_specs=[whole((LAGS, OWN, HALF))] * 2,
            scratch_shapes=[
                pltpu.VMEM((2, DEPTH, 2 * HALF), jnp.bfloat16),
                pltpu.VMEM((2, 2 * FREQ, 2 * HALF), jnp.float32),
                pltpu.VMEM((FREQ * PITCH, HALF), jnp.float32),
                pltpu.VMEM(left.shape, left.dtype),
                pltpu.VMEM((ROWS, FREQ, HALF), jnp.bfloat16),
                pltpu.VMEM((2, BLOCK * XPITCH, HALF), jnp.float32),
                pltpu.VMEM((SHIFTS * BLOCK, HALF), jnp.float32),
                pltpu.VMEM((SHIFTS * BLOCK, HALF), jnp.float32),
                pltpu.SemaphoreType.DMA,
            ],
        ),
        out_shape=[jax.ShapeDtypeStruct((LAGS, OWN, HALF), jnp.bfloat16)] * 2,
        compiler_params=pltpu.CompilerParams(vmem_limit_bytes=VMEM),
        cost_estimate=pl.CostEstimate(flops=30 * 10**9, bytes_accessed=24 << 20, transcendentals=0),
    )(place, x, flags, *tables, left)


def add_kernel(place_ref, added_ref, old_ref, out_ref):
    out_ref[...] = old_ref[...].astype(jnp.float32) + added_ref[...].astype(jnp.float32)


def add_rest_kernel(place_ref, stacks_ref, added_ref, old_ref, out_ref):
    add_kernel(place_ref, added_ref, old_ref, out_ref)


def add_half(place, added, old, stacks=None):
    rows = 201
    first = stacks is None
    column = (lambda place: place[0]) if first else (lambda place: 1 - place[0])
    spec = pl.BlockSpec((rows, OWN, HALF), lambda l, place: (l, 0, column(place)))
    return pl.pallas_call(
        add_kernel if first else add_rest_kernel,
        grid_spec=pltpu.PrefetchScalarGridSpec(
            num_scalar_prefetch=1,
            grid=(pl.cdiv(LAGS, rows),),
            in_specs=([] if first else [pl.BlockSpec(memory_space=pl.ANY)])
            + [pl.BlockSpec((rows, OWN, HALF), lambda l, place: (l, 0, 0)), spec],
            out_specs=spec,
        ),
        out_shape=jax.ShapeDtypeStruct((LAGS, OWN, 2 * HALF), jnp.float32),
        input_output_aliases={} if first else {1: 0},
        compiler_params=pltpu.CompilerParams(vmem_limit_bytes=ADD_VMEM),
        cost_estimate=pl.CostEstimate(flops=LAGS * OWN * HALF, bytes_accessed=13 << 20, transcendentals=0),
    )(place, *([] if first else [stacks]), added, old)


def outgoing_kernel(record_ref, out_ref):
    for i in range(out_ref.shape[0]):
        for core in range(2):
            column = (2 * i + core) * HALF
            piece = record_ref[:, column : column + HALF]
            for chip in range(2):
                out_ref[i, chip, core] = piece


def outgoing(record):
    blocks = record.shape[1] // (2 * HALF)
    steps = 4
    pieces = pl.pallas_call(
        outgoing_kernel,
        grid=(steps,),
        in_specs=[pl.BlockSpec((PIECE, record.shape[1] // steps), lambda i: (0, i))],
        out_specs=pl.BlockSpec((blocks // steps, 2, 2, PIECE, HALF), lambda i: (i, 0, 0, 0, 0)),
        out_shape=jax.ShapeDtypeStruct((blocks, 2, 2, PIECE, HALF), record.dtype),
        compiler_params=pltpu.CompilerParams(vmem_limit_bytes=VMEM),
        cost_estimate=pl.CostEstimate(flops=0, bytes_accessed=5 << 20, transcendentals=0),
    )(record)
    return pieces.reshape(4 * blocks, PIECE, HALF)


def device(x, y, z_low, z_high, core):
    return ((x * 4 + y) * 2 + z_low) * 4 + z_high * 2 + core


def send(value, route):
    places = [(x, y, l, h, c) for x in range(4) for y in range(4) for l in range(2) for h in range(2) for c in range(2)]
    return lax.ppermute(value, ("rcv", "src"), [(device(*place), device(*route(*place))) for place in places])


def near_sources(record, z_low, z_high):
    near = record[:, : 2 * SRC]
    same = jnp.where(z_high == 0, near[:, :SRC], near[:, SRC:])
    other = jnp.where(z_high == 0, near[:, SRC:], near[:, :SRC])
    low = send(same, lambda x, y, l, h, c: (x, y, 1 - l, h, c))
    high = send(other, lambda x, y, l, h, c: (x, y, l, 1 - h, c))
    both = send(other, lambda x, y, l, h, c: (x, y, 1 - l, 1 - h, c))

    def windows(mine, theirs):
        return jnp.where(z_low == 0, jnp.concatenate([mine, theirs], 1), jnp.concatenate([theirs, mine], 1))

    mine, theirs = windows(same, low), windows(high, both)
    return jnp.where(z_high == 0, jnp.stack([mine, theirs]), jnp.stack([theirs, mine]))


def along_y(near):
    return jnp.stack([near] + [send(near, lambda x, y, l, h, c, d=d: (x, y ^ d, l, h, c)) for d in (1, 2, 3)])


def along_x(column):
    plane = jnp.stack([column] + [send(column, lambda x, y, l, h, c, d=d: (x ^ d, y, l, h, c)) for d in (1, 2, 3)])
    return plane.reshape(SUB // 2, 2, PIECE, HALF)


def both_cores(plane, core):
    other = send(plane, lambda x, y, l, h, c: (x, y, l, h, 1 - c))
    rows = jnp.where(core == 0, jnp.stack([plane, other], axis=2), jnp.stack([other, plane], axis=2))
    return rows.reshape(SUB // 2, 4, PIECE, HALF)


def on_device(record, quality, keep_flags, old_stacks):
    row = lax.axis_index("rcv")
    col = lax.axis_index("src")
    core = lax.rem(col, 2)
    chip = lax.div(col, 2)
    z_low = lax.rem(row, 2)
    group = lax.div(row, 2)
    place = jnp.stack([core, group]).astype(jnp.int32)

    pieces = outgoing(record)
    near, pieces = lax.optimization_barrier((near_sources(record, z_low, chip), pieces))
    column, pieces = lax.optimization_barrier((along_y(near), pieces))
    plane = along_x(column)
    receivers = lax.all_to_all(pieces, ("rcv", "src"), split_axis=0, concat_axis=0, tiled=True)
    sources = both_cores(plane, core)

    keep_all = keep_flags.astype(jnp.float32)
    flags = keep_all * quality.astype(jnp.float32)[None, :]
    first_receiver = row * 2 * HALF + core * HALF
    keep_src = lax.dynamic_slice_in_dim(keep_all, chip * SRC, SRC, 1)
    keep_rcv = lax.dynamic_slice_in_dim(keep_all, first_receiver, HALF, 1)
    inverse_count = 1.0 / jnp.maximum(dot(keep_src.T, keep_rcv), 1.0)
    order = lax.bitwise_xor(jnp.arange(SUB // 2, dtype=jnp.int32), group.astype(jnp.int32))
    flags_src = lax.dynamic_slice_in_dim(flags, chip * SRC, SRC, 1).reshape(SUB // 2, 1, 2 * SRC)[order]
    flags_rcv = lax.dynamic_slice_in_dim(flags, first_receiver, HALF, 1).reshape(SUB // 2, 2, HALF)[order]

    left = whiten_sources(sources, flags_src)
    receivers = receivers.reshape(SUB // 2 // PAIRS, PAIRS, 2, 4, PIECE, HALF)
    flags_rcv = flags_rcv.reshape(SUB // 2, 2, 1, HALF)
    away, mine = stack_halves(place, receivers, flags_rcv, left, inverse_count)
    got = lax.ppermute(away, "src", [(0, 1), (1, 0), (2, 3), (3, 2)])
    stacks = add_half(place, mine, old_stacks)
    return add_half(place, got, old_stacks, stacks)


def solution(mesh):
    return jax.shard_map(
        on_device,
        mesh=mesh,
        in_specs=(P(("rcv", "src"), None), P(), P(), P(None, "src", "rcv")),
        out_specs=P(None, "src", "rcv"),
        check_vma=False,
    )
```

```python
import functools
import math

import jax
import jax.numpy as jnp
import numpy as np
from jax import lax
from jax.experimental import pallas as pl
from jax.experimental.pallas import tpu as pltpu
from jax.sharding import PartitionSpec as P

WIN = 400
NFFT = 800
BINS = 401
LARGEST_LAG = 200
LAGS = 401
HALFBAND = 32
SUB = 32
EPSILON = 1e-06

PIECE = WIN // 4
PADDED = 112
DEPTH = 4 * PADDED
FREQ = 416
MIDDLE = 200
EVENS = 48
HALF = 128
SRC = 64
OWN = 32
REACH = 256
SHIFTS = 208
PITCH = 72
SPITCH = 40
ROWS = 2 * SRC
XPITCH = ROWS + 8
BLOCK = 16
PAIRS = 4
VMEM = 60 * 1024 * 1024
ADD_VMEM = 62 * 1024 * 1024


def split(table):
    high = table.astype(jnp.bfloat16)
    low = (table - high.astype(np.float32)).astype(jnp.bfloat16)
    return high, low


def bin_order():
    order = np.full(FREQ, -1)
    order[: MIDDLE + 1] = np.arange(MIDDLE + 1)
    order[SHIFTS : SHIFTS + MIDDLE] = 2 * MIDDLE - np.arange(MIDDLE)
    return order


def forward_table():
    samples = np.arange(WIN)[None, :]
    order = bin_order()
    valid = (order >= 0)[:, None, None]
    phases = (samples * order[:, None] % NFFT) * (2.0 * math.pi / NFFT)
    table = np.zeros((2, FREQ, 4, PADDED), np.float32)
    table[0, :, :, :PIECE] = np.cos(phases).reshape(FREQ, 4, PIECE) * valid
    table[1, :, :, :PIECE] = -np.sin(phases).reshape(FREQ, 4, PIECE) * valid
    high, low = split(table.reshape(2 * FREQ, DEPTH))
    sums = (high.astype(np.float64) + low.astype(np.float64)).sum(axis=1, keepdims=True)
    sums = np.broadcast_to((sums / WIN).astype(np.float32), (2 * FREQ, HALF)).copy()
    return np.concatenate([high, low], axis=1), sums


def piece_order():
    return np.concatenate([np.arange(0, 2 * EVENS, 2), np.arange(1, 2 * EVENS, 2), [96, 98, 97, 99]])


def parity_tables():
    times = np.full((2, REACH), -1)
    pieces = piece_order()
    for j in range(4):
        for parity in range(2):
            times[parity, j * EVENS : (j + 1) * EVENS] = j * PIECE + pieces[parity * EVENS : (parity + 1) * EVENS]
            last = 4 * EVENS + j * BLOCK + 2 * parity
            times[parity, last : last + 2] = j * PIECE + pieces[2 * EVENS + 2 * parity : 2 * EVENS + 2 * parity + 2]
    assert sorted(times[times >= 0]) == list(range(WIN))
    bins = np.arange(SHIFTS)[:, None]
    phases = (times[:, None, :] * bins % NFFT) * (2.0 * math.pi / NFFT)
    valid = (times >= 0)[:, None, :] & (bins <= MIDDLE)
    table = np.concatenate([np.cos(phases) * valid, -np.sin(phases) * valid], axis=1).astype(np.float32)
    high, low = split(table)
    even, odd = (high.astype(np.float64) + low.astype(np.float64)).sum(axis=2, keepdims=True)
    (er, ei), (orr, oi) = (np.split(part, 2) for part in (even, odd))
    sums = np.concatenate([er + orr, er - orr, ei + oi, oi - ei]) / WIN
    sums = np.broadcast_to(sums.astype(np.float32), (2 * FREQ, HALF)).copy()
    return np.concatenate([high, low], axis=2), sums


def band_table():
    order = bin_order()
    columns = (order >= 0)[None, :]
    rows = order.copy()
    rows[SHIFTS + MIDDLE] = MIDDLE
    inside = (np.abs(rows[:, None] - order[None, :]) <= HALFBAND) & columns & (rows >= 0)[:, None]
    counts = np.maximum(inside.sum(axis=1, keepdims=True), 1)
    inverse = np.broadcast_to((1.0 / (2.0 * counts)).astype(np.float32), (FREQ, HALF)).copy()
    near = FREQ - REACH + SHIFTS
    first = np.concatenate([inside[:SHIFTS, :SHIFTS], inside[:SHIFTS, near:]], axis=1)
    halves = np.stack([first, inside[SHIFTS:, FREQ - REACH :]])
    assert halves.sum() == inside.sum()
    return np.concatenate([halves, halves], axis=2).astype(jnp.bfloat16), inverse


def lag_tables():
    shifts = np.arange(LARGEST_LAG + 1)[:, None]
    bins = bin_order()[None, :]
    phases = (shifts * bins % NFFT) * (2.0 * math.pi / NFFT)
    weights = np.where((bins == 0) | (bins == NFFT // 2), 1.0, 2.0) / math.sqrt(NFFT) * (bins >= 0)
    tables = np.zeros((2, SHIFTS, FREQ), np.float32)
    tables[0, : LARGEST_LAG + 1] = weights * np.cos(phases)
    tables[1, : LARGEST_LAG + 1] = -weights * np.sin(phases)
    return tables.astype(jnp.bfloat16)


def dot(a, b):
    return jnp.dot(a, b, preferred_element_type=jnp.float32)


def clear_pad(samples):
    samples[...] = jnp.zeros(samples.shape, samples.dtype)


def transform(pieces, samples, table_ref, spec):
    for g in range(2):
        for j in range(4):
            samples[pl.ds(j * PADDED, PIECE), g * HALF : (g + 1) * HALF] = pieces[g][j][...]
    x = samples[...]
    x = jnp.concatenate([x, x], axis=0)
    for i in range(4):
        rows = pl.ds(i * SHIFTS, SHIFTS)
        spec[rows, :] = dot(table_ref[rows, :], x)
    return spec[:FREQ], spec[FREQ:]


def transform_parities(pieces, samples, table_ref, spec):
    for g in range(2):
        lanes = slice(g * HALF, (g + 1) * HALF)
        for j in range(4):
            last = pieces[g][j][pl.ds(2 * EVENS, PIECE - 2 * EVENS), :]
            for parity in range(2):
                samples[parity, pl.ds(j * EVENS, EVENS), lanes] = pieces[g][j][pl.ds(parity * EVENS, EVENS), :]
                samples[parity, pl.ds(4 * EVENS + j * BLOCK, PIECE - 2 * EVENS), lanes] = last
    for parity in range(2):
        x = samples[parity]
        x = jnp.concatenate([x, x], axis=0)
        for i in range(2):
            rows = pl.ds(i * SHIFTS, SHIFTS)
            spec[parity, rows, :] = dot(table_ref[parity, rows, :], x)
    even_real, even_imag = spec[0, :SHIFTS], spec[0, SHIFTS:]
    odd_real, odd_imag = spec[1, :SHIFTS], spec[1, SHIFTS:]
    real = jnp.concatenate([even_real + odd_real, even_real - odd_real], axis=0)
    imag = jnp.concatenate([even_imag + odd_imag, odd_imag - even_imag], axis=0)
    return real, imag


def whiten_pair(spectrum, flags, sums_ref, band_ref, inverse_ref):
    real, imag = spectrum
    total = real[0:1, :]
    sums = sums_ref[...]
    sums = jnp.concatenate([sums, sums], axis=1)
    real = real - sums[:FREQ] * total
    imag = imag - sums[FREQ:] * total
    power = real * real + imag * imag
    power_high = power.astype(jnp.bfloat16)
    power_low = (power - power_high.astype(jnp.float32)).astype(jnp.bfloat16)
    near = FREQ - REACH + SHIFTS
    first = [rows for part in (power_high, power_low) for rows in (part[:SHIFTS], part[near:])]
    second = [part[FREQ - REACH :] for part in (power_high, power_low)]
    smooth = [dot(band_ref[i], jnp.concatenate(rows, axis=0)) for i, rows in enumerate((first, second))]
    smooth = jnp.concatenate(smooth, axis=0)
    inverse = inverse_ref[...]
    inverse = jnp.concatenate([inverse, inverse], axis=1)
    scale = flags * lax.rsqrt(smooth * inverse + EPSILON)
    return real * scale, imag * scale


def whiten_sources_kernel(
    x_ref, flag_ref, table_ref, sums_ref, band_ref, inverse_ref, out_ref, samples, spec, held
):
    step = pl.program_id(0)

    @pl.when(step == 0)
    def _():
        clear_pad(samples)

    pieces = [[x_ref.at[g, j] for j in range(4)] for g in range(2)]
    flags = jnp.concatenate([flag_ref[0], flag_ref[1]], axis=1)
    spectrum = transform(pieces, samples, table_ref, spec)
    real, imag = whiten_pair(spectrum, flags, sums_ref, band_ref, inverse_ref)
    for g in range(2):
        group = 2 * step + g
        first = pl.ds(group, FREQ, stride=SPITCH)
        second = pl.ds(SUB // 2 + group, FREQ, stride=SPITCH)
        own_real = real[:, g * HALF : (g + 1) * HALF]
        own_imag = imag[:, g * HALF : (g + 1) * HALF]
        held[0, first, :] = own_real
        held[0, second, :] = own_imag
        held[1, first, :] = -own_imag
        held[1, second, :] = own_real

    @pl.when(step == pl.num_programs(0) - 1)
    def _():
        low_lanes = lax.broadcasted_iota(jnp.int32, (SRC, HALF), 1) < HALF // 2

        @pl.loop(0, FREQ // 4)
        def _(quad):
            for part in range(2):
                rows = [
                    held[part, pl.ds(pl.multiple_of((4 * quad + i) * SPITCH, 8), SUB), :] for i in range(4)
                ]
                turned = jnp.concatenate(rows, axis=0).T
                first, second = turned[:SRC], turned[SRC:]
                pairs = (
                    jnp.where(low_lanes, first, pltpu.roll(second, HALF // 2, 1)),
                    jnp.where(low_lanes, pltpu.roll(first, HALF // 2, 1), second),
                )
                for i in range(2):
                    out_ref[2 * quad + i, part * SRC : (part + 1) * SRC] = pairs[i].astype(jnp.bfloat16)


def whole(shape):
    return pl.BlockSpec(shape, lambda *_: (0,) * len(shape))


def whiten_tables(forward):
    return [jnp.asarray(table) for table in (*forward(), *band_table())]


def whiten_cost(groups):
    return pl.CostEstimate(
        flops=groups * 4 * 2 * FREQ * DEPTH * HALF, bytes_accessed=groups * DEPTH * HALF * 6, transcendentals=0
    )


def whiten_sources(x, flags):
    tables = whiten_tables(forward_table)
    return pl.pallas_call(
        whiten_sources_kernel,
        grid=(SUB // 4,),
        in_specs=[
            pl.BlockSpec((2, 4, PIECE, HALF), lambda g: (g, 0, 0, 0)),
            pl.BlockSpec((2, 1, HALF), lambda g: (g, 0, 0)),
        ]
        + [whole(table.shape) for table in tables],
        out_specs=whole((FREQ // 2, ROWS, HALF)),
        out_shape=jax.ShapeDtypeStruct((FREQ // 2, ROWS, HALF), jnp.bfloat16),
        scratch_shapes=[
            pltpu.VMEM((DEPTH, 2 * HALF), jnp.bfloat16),
            pltpu.VMEM((2 * FREQ, 2 * HALF), jnp.float32),
            pltpu.VMEM((2, FREQ * SPITCH, HALF), jnp.float32),
        ],
        compiler_params=pltpu.CompilerParams(vmem_limit_bytes=VMEM),
        cost_estimate=whiten_cost(SUB // 2),
    )(x, flags, *tables)


def lag_pair(pair, real_ref, imag_ref, tables_ref, even, odd):
    real = jnp.concatenate([real_ref[2 * pair], real_ref[2 * pair + 1]], axis=1)
    imag = jnp.concatenate([imag_ref[2 * pair], imag_ref[2 * pair + 1]], axis=1)
    cosine = dot(tables_ref[0], real)
    sine = dot(tables_ref[1], imag)
    for i in range(2):
        rows = pl.ds(2 * pair + i, SHIFTS, stride=BLOCK)
        even[rows, :] = cosine[:, i * HALF : (i + 1) * HALF]
        odd[rows, :] = sine[:, i * HALF : (i + 1) * HALF]


def combine(first, last, count, even, odd, out_ref):
    for m in range(first, last):
        rows = pl.ds(m * BLOCK, BLOCK)
        e, o = even[rows, :], odd[rows, :]
        out_ref[LARGEST_LAG + m] = ((e + o) * count).astype(jnp.bfloat16)
        if m > 0:
            out_ref[LARGEST_LAG - m] = ((e - o) * count).astype(jnp.bfloat16)


def stack_kernel(
    place_ref,
    x_ref,
    flag_ref,
    table_ref,
    sums_ref,
    band_ref,
    inverse_ref,
    tables_ref,
    count_ref,
    left_hbm,
    away_hbm,
    mine_hbm,
    samples,
    spec,
    held,
    left_ref,
    spectra,
    products,
    even,
    odd,
    halves,
    sems,
):
    step = pl.program_id(0)
    core = place_ref[0]
    inner = lax.rem(place_ref[1], PAIRS)
    left_copy = pltpu.make_async_copy(left_hbm, left_ref, sems.at[0])

    @pl.when(step == 0)
    def _():
        left_copy.start()
        clear_pad(samples)

    for p in range(PAIRS):
        source = lax.bitwise_xor(p, inner)
        pieces = [[x_ref.at[source, g, j] for j in range(4)] for g in range(2)]
        flags = jnp.concatenate([flag_ref[p, 0], flag_ref[p, 1]], axis=1)
        spectrum = transform_parities(pieces, samples.at[p % 2], table_ref, spec.at[p % 2])
        real, imag = whiten_pair(spectrum, flags, sums_ref, band_ref, inverse_ref)
        for g in range(2):
            row = g * SUB + step * PAIRS + p
            held[pl.ds(row, FREQ, stride=PITCH), :] = real[:, g * HALF : (g + 1) * HALF]
            held[pl.ds(row + SUB // 2, FREQ, stride=PITCH), :] = imag[:, g * HALF : (g + 1) * HALF]

    @pl.when(step == pl.num_programs(0) - 1)
    def _():
        left_copy.wait()
        zeros = jnp.zeros((2 * SUB, HALF), jnp.bfloat16)

        def receivers(f):
            return held[pl.ds(pl.multiple_of(f * PITCH, 8), 2 * SUB), :].astype(jnp.bfloat16)

        @pl.loop(0, FREQ // (2 * BLOCK))
        def _(outer):
            for side in range(2):
                block = 2 * outer + side
                for pair in range(BLOCK // 2):
                    f = block * BLOCK + 2 * pair
                    first = jnp.concatenate([receivers(f), zeros], axis=1)
                    second = jnp.concatenate([zeros, receivers(f + 1)], axis=1)
                    weights = jnp.concatenate([first[:SUB], second[:SUB], first[SUB:], second[SUB:]], axis=0)
                    product = dot(left_ref[block * (BLOCK // 2) + pair], weights)
                    products[side, pl.ds(2 * pair * XPITCH, ROWS), :] = product[:, :HALF]
                    products[side, pl.ds((2 * pair + 1) * XPITCH, ROWS), :] = product[:, HALF:]
                bins = pl.ds(pl.multiple_of(block * BLOCK, BLOCK), BLOCK)
                for row in range(ROWS):
                    spectra[row, bins, :] = products[side, pl.ds(row, BLOCK, stride=XPITCH), :].astype(jnp.bfloat16)

        groups = [(half, g) for half in range(2) for g in range(OWN // BLOCK)]
        starts = [lax.bitwise_xor(core, 1 - half) * OWN + g * BLOCK for half, g in groups]
        shares = [(LARGEST_LAG + 1) * i // (BLOCK // 2) for i in range(BLOCK // 2 + 1)]
        copies = [
            pltpu.make_async_copy(
                halves.at[i],
                (away_hbm, mine_hbm)[half].at[:, pl.ds(g * BLOCK, BLOCK)],
                sems.at[1 + i],
            )
            for i, (half, g) in enumerate(groups)
        ]

        def finish(i, first, last):
            count = count_ref[pl.ds(pl.multiple_of(starts[i], BLOCK), BLOCK), :]
            combine(first, last, count, even.at[i % 2], odd.at[i % 2], halves.at[i])
            if last > LARGEST_LAG:
                copies[i].start()

        for i, start in enumerate(starts):
            for pair in range(BLOCK // 2):
                lag_pair(
                    pair,
                    spectra.at[pl.ds(start, BLOCK)],
                    spectra.at[pl.ds(SRC + start, BLOCK)],
                    tables_ref,
                    even.at[i % 2],
                    odd.at[i % 2],
                )
                if i > 0:
                    finish(i - 1, shares[pair], shares[pair + 1])
        finish(len(starts) - 1, 0, LARGEST_LAG + 1)
        for copy in copies:
            copy.wait()


def stack_halves(place, x, flags, left, inverse_count):
    tables = whiten_tables(parity_tables) + [jnp.asarray(lag_tables()), inverse_count]
    return pl.pallas_call(
        stack_kernel,
        grid_spec=pltpu.PrefetchScalarGridSpec(
            num_scalar_prefetch=1,
            grid=(SUB // 2 // PAIRS,),
            in_specs=[
                pl.BlockSpec(
                    (None, PAIRS, 2, 4, PIECE, HALF),
                    lambda g, place: (lax.bitwise_xor(g, lax.div(place[1], PAIRS)), 0, 0, 0, 0, 0),
                ),
                pl.BlockSpec((PAIRS, 2, 1, HALF), lambda g, place: (g, 0, 0, 0)),
            ]
            + [whole(table.shape) for table in tables]
            + [pl.BlockSpec(memory_space=pl.ANY)],
            out_specs=[pl.BlockSpec(memory_space=pl.ANY)] * 2,
            scratch_shapes=[
                pltpu.VMEM((2, 2, REACH, 2 * HALF), jnp.bfloat16),
                pltpu.VMEM((2, 2, FREQ, 2 * HALF), jnp.float32),
                pltpu.VMEM((FREQ * PITCH, HALF), jnp.float32),
                pltpu.VMEM(left.shape, left.dtype),
                pltpu.VMEM((ROWS, FREQ, HALF), jnp.bfloat16),
                pltpu.VMEM((2, BLOCK * XPITCH, HALF), jnp.float32),
                pltpu.VMEM((2, SHIFTS * BLOCK, HALF), jnp.float32),
                pltpu.VMEM((2, SHIFTS * BLOCK, HALF), jnp.float32),
                pltpu.VMEM((SRC // BLOCK, LAGS, BLOCK, HALF), jnp.bfloat16),
                pltpu.SemaphoreType.DMA((1 + SRC // BLOCK,)),
            ],
        ),
        out_shape=[jax.ShapeDtypeStruct((LAGS, OWN, HALF), jnp.bfloat16)] * 2,
        compiler_params=pltpu.CompilerParams(vmem_limit_bytes=VMEM),
        cost_estimate=pl.CostEstimate(flops=30 * 10**9, bytes_accessed=24 << 20, transcendentals=0),
    )(place, x, flags, *tables, left)


def add_kernel(place_ref, added_ref, old_ref, out_ref):
    out_ref[...] = old_ref[...].astype(jnp.float32) + added_ref[...].astype(jnp.float32)


def add_rest_kernel(place_ref, stacks_ref, added_ref, old_ref, out_ref):
    add_kernel(place_ref, added_ref, old_ref, out_ref)


def add_half(place, added, old, stacks=None):
    rows = 201
    first = stacks is None
    column = (lambda place: place[0]) if first else (lambda place: 1 - place[0])
    spec = pl.BlockSpec((rows, OWN, HALF), lambda l, place: (l, 0, column(place)))
    return pl.pallas_call(
        add_kernel if first else add_rest_kernel,
        grid_spec=pltpu.PrefetchScalarGridSpec(
            num_scalar_prefetch=1,
            grid=(pl.cdiv(LAGS, rows),),
            in_specs=([] if first else [pl.BlockSpec(memory_space=pl.ANY)])
            + [pl.BlockSpec((rows, OWN, HALF), lambda l, place: (l, 0, 0)), spec],
            out_specs=spec,
        ),
        out_shape=jax.ShapeDtypeStruct((LAGS, OWN, 2 * HALF), jnp.float32),
        input_output_aliases={} if first else {1: 0},
        compiler_params=pltpu.CompilerParams(vmem_limit_bytes=ADD_VMEM),
        cost_estimate=pl.CostEstimate(flops=LAGS * OWN * HALF, bytes_accessed=13 << 20, transcendentals=0),
    )(place, *([] if first else [stacks]), added, old)


def outgoing_kernel(record_ref, order_ref, out_ref):
    for i in range(out_ref.shape[0]):
        for core in range(2):
            column = (2 * i + core) * HALF
            piece = dot(order_ref[...], record_ref[:, column : column + HALF]).astype(record_ref.dtype)
            for chip in range(2):
                out_ref[i, chip, core] = piece


def outgoing(record):
    blocks = record.shape[1] // (2 * HALF)
    steps = 4
    order = (piece_order()[:, None] == np.arange(PIECE)[None, :]).astype(jnp.bfloat16)
    pieces = pl.pallas_call(
        outgoing_kernel,
        grid=(steps,),
        in_specs=[pl.BlockSpec((PIECE, record.shape[1] // steps), lambda i: (0, i)), whole(order.shape)],
        out_specs=pl.BlockSpec((blocks // steps, 2, 2, PIECE, HALF), lambda i: (i, 0, 0, 0, 0)),
        out_shape=jax.ShapeDtypeStruct((blocks, 2, 2, PIECE, HALF), record.dtype),
        compiler_params=pltpu.CompilerParams(vmem_limit_bytes=VMEM),
        cost_estimate=pl.CostEstimate(flops=0, bytes_accessed=5 << 20, transcendentals=0),
    )(record, jnp.asarray(order))
    return pieces.reshape(4 * blocks, PIECE, HALF)


def device(x, y, z_low, z_high, core):
    return ((x * 4 + y) * 2 + z_low) * 4 + z_high * 2 + core


def send(value, route):
    places = [(x, y, l, h, c) for x in range(4) for y in range(4) for l in range(2) for h in range(2) for c in range(2)]
    return lax.ppermute(value, ("rcv", "src"), [(device(*place), device(*route(*place))) for place in places])


def near_sources(record, z_low, z_high):
    near = record[:, : 2 * SRC]
    same = jnp.where(z_high == 0, near[:, :SRC], near[:, SRC:])
    other = jnp.where(z_high == 0, near[:, SRC:], near[:, :SRC])
    low = send(same, lambda x, y, l, h, c: (x, y, 1 - l, h, c))
    high = send(other, lambda x, y, l, h, c: (x, y, l, 1 - h, c))
    both = send(other, lambda x, y, l, h, c: (x, y, 1 - l, 1 - h, c))

    def windows(mine, theirs):
        return jnp.where(z_low == 0, jnp.concatenate([mine, theirs], 1), jnp.concatenate([theirs, mine], 1))

    mine, theirs = windows(same, low), windows(high, both)
    return jnp.where(z_high == 0, jnp.stack([mine, theirs]), jnp.stack([theirs, mine]))


def along_y(near):
    return jnp.stack([near] + [send(near, lambda x, y, l, h, c, d=d: (x, y ^ d, l, h, c)) for d in (1, 2, 3)])


def along_x(column):
    plane = jnp.stack([column] + [send(column, lambda x, y, l, h, c, d=d: (x ^ d, y, l, h, c)) for d in (1, 2, 3)])
    return plane.reshape(SUB // 2, 2, PIECE, HALF)


def both_cores(plane, core):
    other = send(plane, lambda x, y, l, h, c: (x, y, l, h, 1 - c))
    rows = jnp.where(core == 0, jnp.stack([plane, other], axis=2), jnp.stack([other, plane], axis=2))
    return rows.reshape(SUB // 2, 4, PIECE, HALF)


def on_device(record, quality, keep_flags, old_stacks):
    row = lax.axis_index("rcv")
    col = lax.axis_index("src")
    core = lax.rem(col, 2)
    chip = lax.div(col, 2)
    z_low = lax.rem(row, 2)
    group = lax.div(row, 2)
    place = jnp.stack([core, group]).astype(jnp.int32)

    pieces = outgoing(record)
    near, pieces = lax.optimization_barrier((near_sources(record, z_low, chip), pieces))
    column, pieces = lax.optimization_barrier((along_y(near), pieces))
    plane = along_x(column)
    receivers = lax.all_to_all(pieces, ("rcv", "src"), split_axis=0, concat_axis=0, tiled=True)
    sources = both_cores(plane, core)

    keep_all = keep_flags.astype(jnp.float32)
    flags = keep_all * quality.astype(jnp.float32)[None, :]
    first_receiver = row * 2 * HALF + core * HALF
    keep_src = lax.dynamic_slice_in_dim(keep_all, chip * SRC, SRC, 1)
    keep_rcv = lax.dynamic_slice_in_dim(keep_all, first_receiver, HALF, 1)
    inverse_count = 1.0 / jnp.maximum(dot(keep_src.T, keep_rcv), 1.0)
    order = lax.bitwise_xor(jnp.arange(SUB // 2, dtype=jnp.int32), group.astype(jnp.int32))
    flags_src = lax.dynamic_slice_in_dim(flags, chip * SRC, SRC, 1).reshape(SUB // 2, 1, 2 * SRC)[order]
    flags_rcv = lax.dynamic_slice_in_dim(flags, first_receiver, HALF, 1).reshape(SUB // 2, 2, HALF)[order]

    left = whiten_sources(sources, flags_src)
    receivers = receivers.reshape(SUB // 2 // PAIRS, PAIRS, 2, 4, PIECE, HALF)
    flags_rcv = flags_rcv.reshape(SUB // 2, 2, 1, HALF)
    away, mine = stack_halves(place, receivers, flags_rcv, left, inverse_count)
    got = lax.ppermute(away, "src", [(0, 1), (1, 0), (2, 3), (3, 2)])
    stacks = add_half(place, mine, old_stacks)
    return add_half(place, got, old_stacks, stacks)


def solution(mesh):
    return jax.shard_map(
        on_device,
        mesh=mesh,
        in_specs=(P(("rcv", "src"), None), P(), P(), P(None, "src", "rcv")),
        out_specs=P(None, "src", "rcv"),
        check_vma=False,
    )
```

```python
import functools
import math

import jax
import jax.numpy as jnp
import numpy as np
from jax import lax
from jax.experimental import pallas as pl
from jax.experimental.pallas import tpu as pltpu
from jax.sharding import PartitionSpec as P

WIN = 400
NFFT = 800
BINS = 401
LARGEST_LAG = 200
LAGS = 401
HALFBAND = 32
SUB = 32
EPSILON = 1e-06

PIECE = WIN // 4
PADDED = 112
DEPTH = 4 * PADDED
FREQ = 416
MIDDLE = 200
EVENS = 48
HALF = 128
SRC = 64
OWN = 32
REACH = 256
SHIFTS = 208
PITCH = 72
SPITCH = 40
ROWS = 2 * SRC
XPITCH = ROWS + 8
BLOCK = 16
PAIRS = 4
VMEM = 60 * 1024 * 1024
ADD_VMEM = 62 * 1024 * 1024


def split(table):
    high = table.astype(jnp.bfloat16)
    low = (table - high.astype(np.float32)).astype(jnp.bfloat16)
    return high, low


def bin_order():
    order = np.full(FREQ, -1)
    order[: MIDDLE + 1] = np.arange(MIDDLE + 1)
    order[SHIFTS : SHIFTS + MIDDLE] = 2 * MIDDLE - np.arange(MIDDLE)
    return order


def forward_table():
    samples = np.arange(WIN)[None, :]
    order = bin_order()
    valid = (order >= 0)[:, None, None]
    phases = (samples * order[:, None] % NFFT) * (2.0 * math.pi / NFFT)
    table = np.zeros((2, FREQ, 4, PADDED), np.float32)
    table[0, :, :, :PIECE] = np.cos(phases).reshape(FREQ, 4, PIECE) * valid
    table[1, :, :, :PIECE] = -np.sin(phases).reshape(FREQ, 4, PIECE) * valid
    high, low = split(table.reshape(2 * FREQ, DEPTH))
    sums = (high.astype(np.float64) + low.astype(np.float64)).sum(axis=1, keepdims=True)
    sums = np.broadcast_to((sums / WIN).astype(np.float32), (2 * FREQ, HALF)).copy()
    return np.concatenate([high, low], axis=1), sums


def piece_order():
    return np.concatenate([np.arange(0, 2 * EVENS, 2), np.arange(1, 2 * EVENS, 2), [96, 98, 97, 99]])


def parity_tables():
    times = np.full((2, REACH), -1)
    pieces = piece_order()
    for j in range(4):
        for parity in range(2):
            times[parity, j * EVENS : (j + 1) * EVENS] = j * PIECE + pieces[parity * EVENS : (parity + 1) * EVENS]
            last = 4 * EVENS + j * BLOCK + 2 * parity
            times[parity, last : last + 2] = j * PIECE + pieces[2 * EVENS + 2 * parity : 2 * EVENS + 2 * parity + 2]
    assert sorted(times[times >= 0]) == list(range(WIN))
    bins = np.arange(SHIFTS)[:, None]
    phases = (times[:, None, :] * bins % NFFT) * (2.0 * math.pi / NFFT)
    valid = (times >= 0)[:, None, :] & (bins <= MIDDLE)
    table = np.concatenate([np.cos(phases) * valid, -np.sin(phases) * valid], axis=1).astype(np.float32)
    high, low = split(table)
    even, odd = (high.astype(np.float64) + low.astype(np.float64)).sum(axis=2, keepdims=True)
    (er, ei), (orr, oi) = (np.split(part, 2) for part in (even, odd))
    sums = np.concatenate([er + orr, er - orr, ei + oi, oi - ei]) / WIN
    sums = np.broadcast_to(sums.astype(np.float32), (2 * FREQ, HALF)).copy()
    return np.concatenate([high, low], axis=2), sums


def band_table():
    order = bin_order()
    columns = (order >= 0)[None, :]
    rows = order.copy()
    rows[SHIFTS + MIDDLE] = MIDDLE
    inside = (np.abs(rows[:, None] - order[None, :]) <= HALFBAND) & columns & (rows >= 0)[:, None]
    counts = np.maximum(inside.sum(axis=1, keepdims=True), 1)
    inverse = np.broadcast_to((1.0 / (2.0 * counts)).astype(np.float32), (FREQ, HALF)).copy()
    near = FREQ - REACH + SHIFTS
    first = np.concatenate([inside[:SHIFTS, :SHIFTS], inside[:SHIFTS, near:]], axis=1)
    halves = np.stack([first, inside[SHIFTS:, FREQ - REACH :]])
    assert halves.sum() == inside.sum()
    return np.concatenate([halves, halves], axis=2).astype(jnp.bfloat16), inverse


def lag_tables():
    shifts = np.arange(LARGEST_LAG + 1)[:, None]
    bins = bin_order()[None, :]
    phases = (shifts * bins % NFFT) * (2.0 * math.pi / NFFT)
    weights = np.where((bins == 0) | (bins == NFFT // 2), 1.0, 2.0) / math.sqrt(NFFT) * (bins >= 0)
    tables = np.zeros((2, SHIFTS, FREQ), np.float32)
    tables[0, : LARGEST_LAG + 1] = weights * np.cos(phases)
    tables[1, : LARGEST_LAG + 1] = -weights * np.sin(phases)
    return tables.astype(jnp.bfloat16)


def dot(a, b):
    return jnp.dot(a, b, preferred_element_type=jnp.float32)


def clear_pad(samples):
    samples[...] = jnp.zeros(samples.shape, samples.dtype)


def transform(pieces, samples, table_ref, spec):
    for g in range(2):
        for j in range(4):
            samples[pl.ds(j * PADDED, PIECE), g * HALF : (g + 1) * HALF] = pieces[g][j][...]
    x = samples[...]
    x = jnp.concatenate([x, x], axis=0)
    for i in range(4):
        rows = pl.ds(i * SHIFTS, SHIFTS)
        spec[rows, :] = dot(table_ref[rows, :], x)
    return spec[:FREQ], spec[FREQ:]


def transform_parities(pieces, samples, table_ref, spec):
    for g in range(2):
        lanes = slice(g * HALF, (g + 1) * HALF)
        for j in range(4):
            last = pieces[g][j][pl.ds(2 * EVENS, PIECE - 2 * EVENS), :]
            for parity in range(2):
                samples[parity, pl.ds(j * EVENS, EVENS), lanes] = pieces[g][j][pl.ds(parity * EVENS, EVENS), :]
                samples[parity, pl.ds(4 * EVENS + j * BLOCK, PIECE - 2 * EVENS), lanes] = last
    for parity in range(2):
        x = samples[parity]
        x = jnp.concatenate([x, x], axis=0)
        for i in range(2):
            rows = pl.ds(i * SHIFTS, SHIFTS)
            spec[parity, rows, :] = dot(table_ref[parity, rows, :], x)
    even_real, even_imag = spec[0, :SHIFTS], spec[0, SHIFTS:]
    odd_real, odd_imag = spec[1, :SHIFTS], spec[1, SHIFTS:]
    real = jnp.concatenate([even_real + odd_real, even_real - odd_real], axis=0)
    imag = jnp.concatenate([even_imag + odd_imag, odd_imag - even_imag], axis=0)
    return real, imag


def whiten_pair(spectrum, flags, sums_ref, band_ref, inverse_ref):
    real, imag = spectrum
    total = real[0:1, :]
    sums = sums_ref[...]
    sums = jnp.concatenate([sums, sums], axis=1)
    real = real - sums[:FREQ] * total
    imag = imag - sums[FREQ:] * total
    power = real * real + imag * imag
    power_high = power.astype(jnp.bfloat16)
    power_low = (power - power_high.astype(jnp.float32)).astype(jnp.bfloat16)
    near = FREQ - REACH + SHIFTS
    first = [rows for part in (power_high, power_low) for rows in (part[:SHIFTS], part[near:])]
    second = [part[FREQ - REACH :] for part in (power_high, power_low)]
    smooth = [dot(band_ref[i], jnp.concatenate(rows, axis=0)) for i, rows in enumerate((first, second))]
    smooth = jnp.concatenate(smooth, axis=0)
    inverse = inverse_ref[...]
    inverse = jnp.concatenate([inverse, inverse], axis=1)
    scale = flags * lax.rsqrt(smooth * inverse + EPSILON)
    return real * scale, imag * scale


def whiten_sources_kernel(
    x_ref, flag_ref, table_ref, sums_ref, band_ref, inverse_ref, out_ref, samples, spec, held
):
    step = pl.program_id(0)

    @pl.when(step == 0)
    def _():
        clear_pad(samples)

    pieces = [[x_ref.at[g, j] for j in range(4)] for g in range(2)]
    flags = jnp.concatenate([flag_ref[0], flag_ref[1]], axis=1)
    spectrum = transform(pieces, samples, table_ref, spec)
    real, imag = whiten_pair(spectrum, flags, sums_ref, band_ref, inverse_ref)
    for g in range(2):
        group = 2 * step + g
        first = pl.ds(group, FREQ, stride=SPITCH)
        second = pl.ds(SUB // 2 + group, FREQ, stride=SPITCH)
        own_real = real[:, g * HALF : (g + 1) * HALF]
        own_imag = imag[:, g * HALF : (g + 1) * HALF]
        held[0, first, :] = own_real
        held[0, second, :] = own_imag
        held[1, first, :] = -own_imag
        held[1, second, :] = own_real

    @pl.when(step == pl.num_programs(0) - 1)
    def _():
        low_lanes = lax.broadcasted_iota(jnp.int32, (SRC, HALF), 1) < HALF // 2
        unit = lax.broadcasted_iota(jnp.int32, (HALF, HALF), 0) == lax.broadcasted_iota(jnp.int32, (HALF, HALF), 1)
        unit = unit.astype(jnp.bfloat16)

        @pl.loop(0, FREQ // 4, unroll=4)
        def _(quad):
            rows = [
                held[part, pl.ds(pl.multiple_of((4 * quad + i) * SPITCH, 8), SUB), :]
                for part in range(2)
                for i in range(4)
            ]
            rows = jnp.concatenate(rows, axis=0).astype(jnp.bfloat16)
            turned = lax.dot_general(unit, rows, (((1,), (1,)), ((), ())), preferred_element_type=jnp.float32)
            for part in range(2):
                first, second = (
                    turned[i * SRC : (i + 1) * SRC, part * HALF : (part + 1) * HALF] for i in range(2)
                )
                pairs = (
                    jnp.where(low_lanes, first, pltpu.roll(second, HALF // 2, 1)),
                    jnp.where(low_lanes, pltpu.roll(first, HALF // 2, 1), second),
                )
                for i in range(2):
                    out_ref[2 * quad + i, part * SRC : (part + 1) * SRC] = pairs[i].astype(jnp.bfloat16)


def whole(shape):
    return pl.BlockSpec(shape, lambda *_: (0,) * len(shape))


def whiten_tables(forward):
    return [jnp.asarray(table) for table in (*forward(), *band_table())]


def whiten_cost(groups):
    return pl.CostEstimate(
        flops=groups * 4 * 2 * FREQ * DEPTH * HALF, bytes_accessed=groups * DEPTH * HALF * 6, transcendentals=0
    )


def whiten_sources(x, flags):
    tables = whiten_tables(forward_table)
    return pl.pallas_call(
        whiten_sources_kernel,
        grid=(SUB // 4,),
        in_specs=[
            pl.BlockSpec((2, 4, PIECE, HALF), lambda g: (g, 0, 0, 0)),
            pl.BlockSpec((2, 1, HALF), lambda g: (g, 0, 0)),
        ]
        + [whole(table.shape) for table in tables],
        out_specs=whole((FREQ // 2, ROWS, HALF)),
        out_shape=jax.ShapeDtypeStruct((FREQ // 2, ROWS, HALF), jnp.bfloat16),
        scratch_shapes=[
            pltpu.VMEM((DEPTH, 2 * HALF), jnp.bfloat16),
            pltpu.VMEM((2 * FREQ, 2 * HALF), jnp.float32),
            pltpu.VMEM((2, (FREQ + 1) * SPITCH, HALF), jnp.float32),
        ],
        compiler_params=pltpu.CompilerParams(vmem_limit_bytes=VMEM),
        cost_estimate=whiten_cost(SUB // 2),
    )(x, flags, *tables)


def lag_pair(pair, real_ref, imag_ref, tables_ref, even, odd):
    real = jnp.concatenate([real_ref[2 * pair], real_ref[2 * pair + 1]], axis=1)
    imag = jnp.concatenate([imag_ref[2 * pair], imag_ref[2 * pair + 1]], axis=1)
    cosine = dot(tables_ref[0], real)
    sine = dot(tables_ref[1], imag)
    for i in range(2):
        rows = pl.ds(2 * pair + i, SHIFTS, stride=BLOCK)
        even[rows, :] = cosine[:, i * HALF : (i + 1) * HALF]
        odd[rows, :] = sine[:, i * HALF : (i + 1) * HALF]


def combine(first, last, count, even, odd, out_ref):
    for m in range(first, last):
        rows = pl.ds(m * BLOCK, BLOCK)
        e, o = even[rows, :], odd[rows, :]
        out_ref[LARGEST_LAG + m] = ((e + o) * count).astype(jnp.bfloat16)
        if m > 0:
            out_ref[LARGEST_LAG - m] = ((e - o) * count).astype(jnp.bfloat16)


def stack_kernel(
    place_ref,
    x_ref,
    flag_ref,
    table_ref,
    sums_ref,
    band_ref,
    inverse_ref,
    tables_ref,
    count_ref,
    left_hbm,
    away_hbm,
    mine_hbm,
    samples,
    spec,
    held,
    left_ref,
    spectra,
    products,
    even,
    odd,
    halves,
    sems,
):
    step = pl.program_id(0)
    core = place_ref[0]
    inner = lax.rem(place_ref[1], PAIRS)
    left_copy = pltpu.make_async_copy(left_hbm, left_ref, sems.at[0])

    @pl.when(step == 0)
    def _():
        left_copy.start()
        clear_pad(samples)

    for p in range(PAIRS):
        source = lax.bitwise_xor(p, inner)
        pieces = [[x_ref.at[source, g, j] for j in range(4)] for g in range(2)]
        flags = jnp.concatenate([flag_ref[p, 0], flag_ref[p, 1]], axis=1)
        spectrum = transform_parities(pieces, samples.at[p % 2], table_ref, spec.at[p % 2])
        real, imag = whiten_pair(spectrum, flags, sums_ref, band_ref, inverse_ref)
        for g in range(2):
            row = g * SUB + step * PAIRS + p
            held[pl.ds(row, FREQ, stride=PITCH), :] = real[:, g * HALF : (g + 1) * HALF]
            held[pl.ds(row + SUB // 2, FREQ, stride=PITCH), :] = imag[:, g * HALF : (g + 1) * HALF]

    @pl.when(step == pl.num_programs(0) - 1)
    def _():
        left_copy.wait()
        zeros = jnp.zeros((2 * SUB, HALF), jnp.bfloat16)

        def receivers(f):
            return held[pl.ds(pl.multiple_of(f * PITCH, 8), 2 * SUB), :].astype(jnp.bfloat16)

        @pl.loop(0, FREQ // (2 * BLOCK))
        def _(outer):
            for side in range(2):
                block = 2 * outer + side
                for pair in range(BLOCK // 2):
                    f = block * BLOCK + 2 * pair
                    first = jnp.concatenate([receivers(f), zeros], axis=1)
                    second = jnp.concatenate([zeros, receivers(f + 1)], axis=1)
                    weights = jnp.concatenate([first[:SUB], second[:SUB], first[SUB:], second[SUB:]], axis=0)
                    product = dot(left_ref[block * (BLOCK // 2) + pair], weights)
                    products[side, pl.ds(2 * pair * XPITCH, ROWS), :] = product[:, :HALF]
                    products[side, pl.ds((2 * pair + 1) * XPITCH, ROWS), :] = product[:, HALF:]
                bins = pl.ds(pl.multiple_of(block * BLOCK, BLOCK), BLOCK)
                for row in range(ROWS):
                    spectra[row, bins, :] = products[side, pl.ds(row, BLOCK, stride=XPITCH), :].astype(jnp.bfloat16)

        groups = [(half, g) for half in range(2) for g in range(OWN // BLOCK)]
        starts = [lax.bitwise_xor(core, 1 - half) * OWN + g * BLOCK for half, g in groups]
        shares = [(LARGEST_LAG + 1) * i // (BLOCK // 2) for i in range(BLOCK // 2 + 1)]
        copies = [
            pltpu.make_async_copy(
                halves.at[i],
                (away_hbm, mine_hbm)[half].at[:, pl.ds(g * BLOCK, BLOCK)],
                sems.at[1 + i],
            )
            for i, (half, g) in enumerate(groups)
        ]

        def finish(i, first, last):
            count = count_ref[pl.ds(pl.multiple_of(starts[i], BLOCK), BLOCK), :]
            combine(first, last, count, even.at[i % 2], odd.at[i % 2], halves.at[i])
            if last > LARGEST_LAG:
                copies[i].start()

        for i, start in enumerate(starts):
            for pair in range(BLOCK // 2):
                lag_pair(
                    pair,
                    spectra.at[pl.ds(start, BLOCK)],
                    spectra.at[pl.ds(SRC + start, BLOCK)],
                    tables_ref,
                    even.at[i % 2],
                    odd.at[i % 2],
                )
                if i > 0:
                    finish(i - 1, shares[pair], shares[pair + 1])
        finish(len(starts) - 1, 0, LARGEST_LAG + 1)
        for copy in copies:
            copy.wait()


def stack_halves(place, x, flags, left, inverse_count):
    tables = whiten_tables(parity_tables) + [jnp.asarray(lag_tables()), inverse_count]
    return pl.pallas_call(
        stack_kernel,
        grid_spec=pltpu.PrefetchScalarGridSpec(
            num_scalar_prefetch=1,
            grid=(SUB // 2 // PAIRS,),
            in_specs=[
                pl.BlockSpec(
                    (None, PAIRS, 2, 4, PIECE, HALF),
                    lambda g, place: (lax.bitwise_xor(g, lax.div(place[1], PAIRS)), 0, 0, 0, 0, 0),
                ),
                pl.BlockSpec((PAIRS, 2, 1, HALF), lambda g, place: (g, 0, 0, 0)),
            ]
            + [whole(table.shape) for table in tables]
            + [pl.BlockSpec(memory_space=pl.ANY)],
            out_specs=[pl.BlockSpec(memory_space=pl.ANY)] * 2,
            scratch_shapes=[
                pltpu.VMEM((2, 2, REACH, 2 * HALF), jnp.bfloat16),
                pltpu.VMEM((2, 2, FREQ, 2 * HALF), jnp.float32),
                pltpu.VMEM(((FREQ + 1) * PITCH, HALF), jnp.float32),
                pltpu.VMEM(left.shape, left.dtype),
                pltpu.VMEM((ROWS, FREQ, HALF), jnp.bfloat16),
                pltpu.VMEM((2, (BLOCK + 1) * XPITCH, HALF), jnp.float32),
                pltpu.VMEM((2, (SHIFTS + 1) * BLOCK, HALF), jnp.float32),
                pltpu.VMEM((2, (SHIFTS + 1) * BLOCK, HALF), jnp.float32),
                pltpu.VMEM((SRC // BLOCK, LAGS, BLOCK, HALF), jnp.bfloat16),
                pltpu.SemaphoreType.DMA((1 + SRC // BLOCK,)),
            ],
        ),
        out_shape=[jax.ShapeDtypeStruct((LAGS, OWN, HALF), jnp.bfloat16)] * 2,
        compiler_params=pltpu.CompilerParams(vmem_limit_bytes=VMEM),
        cost_estimate=pl.CostEstimate(flops=30 * 10**9, bytes_accessed=24 << 20, transcendentals=0),
    )(place, x, flags, *tables, left)


def add_kernel(place_ref, added_ref, old_ref, out_ref):
    out_ref[...] = old_ref[...].astype(jnp.float32) + added_ref[...].astype(jnp.float32)


def add_rest_kernel(place_ref, stacks_ref, added_ref, old_ref, out_ref):
    add_kernel(place_ref, added_ref, old_ref, out_ref)


def add_half(place, added, old, stacks=None):
    rows = 201
    first = stacks is None
    column = (lambda place: place[0]) if first else (lambda place: 1 - place[0])
    spec = pl.BlockSpec((rows, OWN, HALF), lambda l, place: (l, 0, column(place)))
    return pl.pallas_call(
        add_kernel if first else add_rest_kernel,
        grid_spec=pltpu.PrefetchScalarGridSpec(
            num_scalar_prefetch=1,
            grid=(pl.cdiv(LAGS, rows),),
            in_specs=([] if first else [pl.BlockSpec(memory_space=pl.ANY)])
            + [pl.BlockSpec((rows, OWN, HALF), lambda l, place: (l, 0, 0)), spec],
            out_specs=spec,
        ),
        out_shape=jax.ShapeDtypeStruct((LAGS, OWN, 2 * HALF), jnp.float32),
        input_output_aliases={} if first else {1: 0},
        compiler_params=pltpu.CompilerParams(vmem_limit_bytes=ADD_VMEM),
        cost_estimate=pl.CostEstimate(flops=LAGS * OWN * HALF, bytes_accessed=13 << 20, transcendentals=0),
    )(place, *([] if first else [stacks]), added, old)


def outgoing_kernel(record_ref, order_ref, out_ref):
    for i in range(out_ref.shape[0]):
        for core in range(2):
            column = (2 * i + core) * HALF
            piece = dot(order_ref[...], record_ref[:, column : column + HALF]).astype(record_ref.dtype)
            for chip in range(2):
                out_ref[i, chip, core] = piece


def outgoing(record):
    blocks = record.shape[1] // (2 * HALF)
    steps = 4
    order = (piece_order()[:, None] == np.arange(PIECE)[None, :]).astype(jnp.bfloat16)
    pieces = pl.pallas_call(
        outgoing_kernel,
        grid=(steps,),
        in_specs=[pl.BlockSpec((PIECE, record.shape[1] // steps), lambda i: (0, i)), whole(order.shape)],
        out_specs=pl.BlockSpec((blocks // steps, 2, 2, PIECE, HALF), lambda i: (i, 0, 0, 0, 0)),
        out_shape=jax.ShapeDtypeStruct((blocks, 2, 2, PIECE, HALF), record.dtype),
        compiler_params=pltpu.CompilerParams(vmem_limit_bytes=VMEM),
        cost_estimate=pl.CostEstimate(flops=0, bytes_accessed=5 << 20, transcendentals=0),
    )(record, jnp.asarray(order))
    return pieces.reshape(4 * blocks, PIECE, HALF)


def device(x, y, z_low, z_high, core):
    return ((x * 4 + y) * 2 + z_low) * 4 + z_high * 2 + core


def send(value, route):
    places = [(x, y, l, h, c) for x in range(4) for y in range(4) for l in range(2) for h in range(2) for c in range(2)]
    return lax.ppermute(value, ("rcv", "src"), [(device(*place), device(*route(*place))) for place in places])


def near_sources(record, z_low, z_high):
    near = record[:, : 2 * SRC]
    same = jnp.where(z_high == 0, near[:, :SRC], near[:, SRC:])
    other = jnp.where(z_high == 0, near[:, SRC:], near[:, :SRC])
    low = send(same, lambda x, y, l, h, c: (x, y, 1 - l, h, c))
    high = send(other, lambda x, y, l, h, c: (x, y, l, 1 - h, c))
    both = send(other, lambda x, y, l, h, c: (x, y, 1 - l, 1 - h, c))

    def windows(mine, theirs):
        return jnp.where(z_low == 0, jnp.concatenate([mine, theirs], 1), jnp.concatenate([theirs, mine], 1))

    mine, theirs = windows(same, low), windows(high, both)
    return jnp.where(z_high == 0, jnp.stack([mine, theirs]), jnp.stack([theirs, mine]))


def first_round(near):
    def route(d):
        return lambda x, y, l, h, c: (x, y ^ d, l, h, c) if c == 0 else (x ^ d, y, l, h, c)

    return jnp.stack([near] + [send(near, route(d)) for d in (1, 2, 3)])


def second_round(line, core):
    def route(d):
        return lambda x, y, l, h, c: (x ^ d, y, l, h, c) if c == 0 else (x, y ^ d, l, h, c)

    plane = jnp.stack([line] + [send(line, route(d)) for d in (1, 2, 3)])
    plane = jnp.where(core == 0, plane, plane.swapaxes(0, 1))
    return plane.reshape(SUB // 2, 2, PIECE, HALF)


def both_cores(plane, core):
    other = send(plane, lambda x, y, l, h, c: (x, y, l, h, 1 - c))
    rows = jnp.where(core == 0, jnp.stack([plane, other], axis=2), jnp.stack([other, plane], axis=2))
    return rows.reshape(SUB // 2, 4, PIECE, HALF)


def on_device(record, quality, keep_flags, old_stacks):
    row = lax.axis_index("rcv")
    col = lax.axis_index("src")
    core = lax.rem(col, 2)
    chip = lax.div(col, 2)
    z_low = lax.rem(row, 2)
    group = lax.div(row, 2)
    place = jnp.stack([core, group]).astype(jnp.int32)

    pieces = outgoing(record)
    near, pieces = lax.optimization_barrier((near_sources(record, z_low, chip), pieces))
    line, pieces = lax.optimization_barrier((first_round(near), pieces))
    plane = second_round(line, core)
    receivers = lax.all_to_all(pieces, ("rcv", "src"), split_axis=0, concat_axis=0, tiled=True)
    sources = both_cores(plane, core)

    keep_all = keep_flags.astype(jnp.float32)
    flags = keep_all * quality.astype(jnp.float32)[None, :]
    first_receiver = row * 2 * HALF + core * HALF
    keep_src = lax.dynamic_slice_in_dim(keep_all, chip * SRC, SRC, 1)
    keep_rcv = lax.dynamic_slice_in_dim(keep_all, first_receiver, HALF, 1)
    inverse_count = 1.0 / jnp.maximum(dot(keep_src.T, keep_rcv), 1.0)
    order = lax.bitwise_xor(jnp.arange(SUB // 2, dtype=jnp.int32), group.astype(jnp.int32))
    flags_src = lax.dynamic_slice_in_dim(flags, chip * SRC, SRC, 1).reshape(SUB // 2, 1, 2 * SRC)[order]
    flags_rcv = lax.dynamic_slice_in_dim(flags, first_receiver, HALF, 1).reshape(SUB // 2, 2, HALF)[order]

    left = whiten_sources(sources, flags_src)
    receivers = receivers.reshape(SUB // 2 // PAIRS, PAIRS, 2, 4, PIECE, HALF)
    flags_rcv = flags_rcv.reshape(SUB // 2, 2, 1, HALF)
    away, mine = stack_halves(place, receivers, flags_rcv, left, inverse_count)
    got = lax.ppermute(away, "src", [(0, 1), (1, 0), (2, 3), (3, 2)])
    stacks = add_half(place, mine, old_stacks)
    return add_half(place, got, old_stacks, stacks)


def solution(mesh):
    return jax.shard_map(
        on_device,
        mesh=mesh,
        in_specs=(P(("rcv", "src"), None), P(), P(), P(None, "src", "rcv")),
        out_specs=P(None, "src", "rcv"),
        check_vma=False,
    )
```
